32 devices in a mesh: clips: 2 (over y), seq: 4 (over z), cache: 2 (over x), head: 2 (over core).
Axes of the slice: x: 2, y: 2, z: 4, core: 2. Of those that a mesh axis runs over, the one named last changes fastest.
Arguments:
- queries: bfloat16 [3072, 6144], P(('clips', 'seq'), ('cache', 'head')), parts along dimension 0, may hold values from -5 to 5
- keys: bfloat16 [3072, 6144], P(('clips', 'seq'), ('cache', 'head')), parts along dimension 0, may hold values from -5 to 5
- values: bfloat16 [3072, 6144], P(('clips', 'seq'), ('cache', 'head')), parts along dimension 0, may hold values from -6 to 6
- frame_ids: int32 [3072], P(('clips', 'seq')), parts along dimension 0, may hold values from 0 to 7, never falling along the last dimension, each value on 1 to 384 neighbouring positions
- past_keys: bfloat16 [32, 64, 6144], P(('clips', 'seq'), None, ('cache', 'head')), parts along dimension 0, may hold values from -6 to 6
- past_values: bfloat16 [32, 64, 6144], P(('clips', 'seq'), None, ('cache', 'head')), parts along dimension 0, may hold values from -6 to 6
- block_home: int32 [32], P('clips'), parts along dimension 0, may hold values from 0 to 15, as said below
- windows: int32 [8, 4], P('clips'), parts along dimension 0, may hold values from 0 to 15, as said below
- window_len: int32 [8], P('clips'), parts along dimension 0, may hold values from 3 to 4, as said below
Outputs:
- attended: bfloat16 [3072, 6144], P(('clips', 'seq'), ('cache', 'head')), parts along dimension 0
The draws below stay inside these ranges and needn't reach their ends.
There are 2 independent parts, one for each index of `clips`. The reference program is written for one: setup_inputs(seed, part) draws one part's arguments, and reference() takes and returns one part's arrays. A program takes and returns all parts, laid end to end along the dimension named above; each array names one. Nothing has to cross between parts.
Inputs may be any that keep to these rules, and one draw needn't show every extreme that they name: `block_home`: a random order of the 16 storage rows. `windows`: each row holds 4 different past blocks; among the live ones of a row at most 2 have block_home in one owner's range owner * 4 to owner * 4 + 3, and some row reaches 2. `window_len`: some shard has all 4 entries live.
All inputs are finite; a program needn't handle non-finite values.
Results may differ from the reference program's by a relative error of at most 0.006.
Values may be sent and summed in bfloat16 or wider, within the bound.
A program may use at most 64 MiB of HBM per device.

```python
import math
import jax
import jax.numpy as jnp
import numpy as np
from jax import lax

HEADS = 48
HEAD_DIM = 128
TOK_DEV = 384
PB_DEV = 4
BLK = 64
CAP = 2
TOKENS = 1536
NPB = 16
WIN = 4
FRAMES = 8
N_SEQ = 4


def shared_home(key):
    return jax.random.permutation(key, NPB).astype(jnp.int32)


def draw_queries(key, part):
    key = jax.random.fold_in(key, 11)
    drawn = jnp.clip(jax.random.normal(key, (TOKENS, HEADS * HEAD_DIM)), -5.0, 5.0)
    return drawn.astype(jnp.bfloat16)


def draw_keys(key, part):
    key = jax.random.fold_in(key, 12)
    drawn = jnp.clip(jax.random.normal(key, (TOKENS, HEADS * HEAD_DIM)), -5.0, 5.0)
    return drawn.astype(jnp.bfloat16)


def draw_block_home(key, part):
    home_rows = shared_home(key)
    return home_rows


def draw_windows(key, part):
    home_rows = shared_home(key)
    key = jax.random.fold_in(key, 13)
    inverse = jnp.zeros((NPB,), jnp.int32).at[home_rows].set(jnp.arange(NPB, dtype=jnp.int32))
    shard_keys = jax.random.split(key, N_SEQ)

    def one_list(shard_key):
        first_key, second_key, third_key = jax.random.split(shard_key, 3)
        owners = jax.random.permutation(first_key, N_SEQ).astype(jnp.int32)
        offsets = jax.random.randint(second_key, (N_SEQ,), 0, PB_DEV)
        owner_of = jnp.repeat(owners, CAP)
        within = jnp.tile(jnp.arange(CAP, dtype=jnp.int32), N_SEQ)
        storage = owner_of * PB_DEV + (offsets[owner_of] + within) % PB_DEV
        order = jnp.concatenate([jnp.arange(2, dtype=jnp.int32), 2 + jax.random.permutation(third_key, N_SEQ * CAP - 2).astype(jnp.int32)])
        return inverse[storage[order][:WIN]]
    return jax.vmap(one_list)(shard_keys).astype(jnp.int32)


def draw_window_len(key, part):
    key = jax.random.fold_in(key, 14)
    first_key, second_key = jax.random.split(key)
    lowest = WIN - 3 * WIN // 8
    picked = jax.random.randint(first_key, (N_SEQ,), 0, WIN - lowest + 1)
    lengths = lowest + picked
    forced = jax.random.randint(second_key, (), 0, N_SEQ)
    shard_ids = jnp.arange(N_SEQ)
    lengths = jnp.where(shard_ids == (forced + 1) % N_SEQ, lowest, lengths)
    lengths = jnp.where(shard_ids == forced, WIN, lengths)
    return lengths.astype(jnp.int32)


def block_scale(own_key, dims, cuts, smallest, top_value):
    loudness, own = 1.0, jax.random.fold_in(own_key, 6)
    for axis_at, parts in cuts:
        heights = jnp.exp(jax.random.uniform(jax.random.fold_in(own, axis_at), (parts,), jnp.float32, smallest / len(cuts), top_value / len(cuts)))
        loudness = loudness * jnp.repeat(heights, dims[axis_at] // parts).reshape([-1 if axis == axis_at else 1 for axis in range(len(dims))])
    return loudness


def profile(number_of, total, bound, slope):
    loads = [(1 << 20) // math.isqrt(rank ** slope) + 1 for rank in range(2, number_of + 1)]
    rest, holding = total - bound - (number_of - 1), [1] * (number_of - 1)
    while rest > 0:
        candidates = [i for i in range(number_of - 1) if holding[i] < bound]
        mass, budget = sum([loads[i] for i in candidates]), rest
        for i in candidates:
            extra = min(bound - holding[i], max(1, budget * loads[i] // mass), rest)
            holding[i] = holding[i] + extra
            rest = rest - extra
    return np.array([bound] + holding)


def ragged_sizes(key, count, total, reach, slope):
    if count == 2:
        one = jax.random.randint(key, (), max(1, total - reach), min(reach, total - 1) + 1)
        return jnp.stack([one, total - one])
    sizes = jnp.asarray(profile(count, total, reach, slope), jnp.int32)
    twos = (count - 1) // 2
    source_of, taker = sizes[1:1 + 2 * twos:2], sizes[2:2 + 2 * twos:2]
    margin = jnp.minimum(source_of - 1, reach - taker)
    moved = jax.random.randint(jax.random.fold_in(key, 1), (twos,), 0, 1 << 20) % (margin + 1)
    sizes = sizes.at[1:1 + 2 * twos:2].set(source_of - moved).at[2:2 + 2 * twos:2].set(taker + moved)
    return sizes[jax.random.permutation(jax.random.fold_in(key, 2), count)]


def bell_draw(stream_key, extent, scale, limit, shards=(), held_as=jnp.bfloat16):
    entries = scale * jax.random.normal(stream_key, extent, jnp.float32)
    if shards:
        entries = entries * block_scale(stream_key, extent, shards, -0.22, 0.18)
    return jnp.clip(entries, -limit, limit).astype(held_as)


def setup_inputs(seed: int = 0, part: int = 0) -> dict:
    arg_keys = jax.random.split(jax.random.key(seed), 10)
    part_keys = jax.random.split(jax.random.fold_in(arg_keys[9], part), 10)
    queries = draw_queries(jax.random.fold_in(jax.random.fold_in(arg_keys[9], part), 71), part)
    keys = draw_keys(jax.random.fold_in(jax.random.fold_in(arg_keys[9], part), 71), part)
    values = bell_draw(part_keys[2], (TOKENS, HEADS * HEAD_DIM), 1.0, 6.0, ((0, 4), (1, 4)))
    frame_ids = jnp.searchsorted(jnp.cumsum(ragged_sizes(part_keys[3], FRAMES, TOKENS, TOK_DEV, 1)), jnp.arange(TOKENS), side="right").astype(jnp.int32)
    past_keys = bell_draw(part_keys[4], (NPB, BLK, HEADS * HEAD_DIM), 1.0, 6.0, ((0, 4), (2, 4)))
    past_values = bell_draw(part_keys[5], (NPB, BLK, HEADS * HEAD_DIM), 1.0, 6.0, ((0, 4), (2, 4)))
    block_home = draw_block_home(jax.random.fold_in(jax.random.fold_in(arg_keys[9], part), 71), part)
    windows = draw_windows(jax.random.fold_in(jax.random.fold_in(arg_keys[9], part), 71), part)
    window_len = draw_window_len(jax.random.fold_in(jax.random.fold_in(arg_keys[9], part), 71), part)
    return dict(queries=queries, keys=keys, values=values, frame_ids=frame_ids, past_keys=past_keys, past_values=past_values, block_home=block_home, windows=windows, window_len=window_len)


def reference(queries, keys, values, frame_ids, past_keys, past_values, block_home, windows, window_len):
    score_scale = HEAD_DIM ** -0.5
    all_keys = keys.reshape(TOKENS, HEADS, HEAD_DIM)
    all_values = values.reshape(TOKENS, HEADS, HEAD_DIM)

    def one_shard(shard):
        shard_queries = lax.dynamic_slice_in_dim(queries, shard * TOK_DEV, TOK_DEV, 0).reshape(TOK_DEV, HEADS, HEAD_DIM)
        query_frames = lax.dynamic_slice_in_dim(frame_ids, shard * TOK_DEV, TOK_DEV, 0)
        row_ids = block_home[windows[shard]]
        live_slots = jnp.arange(WIN) < window_len[shard]
        past_k = past_keys[row_ids].reshape(WIN * BLK, HEADS, HEAD_DIM)
        past_v = past_values[row_ids].reshape(WIN * BLK, HEADS, HEAD_DIM)
        live_keys = jnp.broadcast_to(jnp.repeat(live_slots, BLK)[None, :], (TOK_DEV, WIN * BLK))
        key_mask = jnp.concatenate([frame_ids[None, :] <= query_frames[:, None], live_keys], axis=1)
        joined_k = jnp.concatenate([all_keys, past_k], axis=0).transpose(1, 0, 2)
        joined_v = jnp.concatenate([all_values, past_v], axis=0).transpose(1, 0, 2)

        def head_attend(items):
            head_q, head_k, head_v = items
            scores = jnp.dot(head_q, head_k.T, preferred_element_type=jnp.float32) * score_scale
            scores = jnp.where(key_mask, scores, -jnp.inf)
            row_max = jnp.max(scores, axis=1, keepdims=True)
            weights = jnp.exp(scores - row_max)
            total = jnp.sum(weights, axis=1, keepdims=True)
            weighted = jnp.dot(weights.astype(jnp.bfloat16), head_v, preferred_element_type=jnp.float32)
            return (weighted / total).astype(jnp.bfloat16)

        per_head = lax.map(head_attend, (shard_queries.transpose(1, 0, 2), joined_k, joined_v))
        return per_head.transpose(1, 0, 2).reshape(TOK_DEV, HEADS * HEAD_DIM)

    return lax.map(one_shard, jnp.arange(N_SEQ)).reshape(TOKENS, HEADS * HEAD_DIM)
```

```python
import functools
import math

import jax
import jax.numpy as jnp
from jax import lax
from jax.experimental import pallas as pl
from jax.experimental.pallas import tpu as pltpu
from jax.sharding import PartitionSpec as P

HEAD_DIM = 128


masked_score = -1e30


def shifted(block, axis, distance):
    devices = range(lax.axis_size(axis))
    route = [((i - distance) % len(devices), i) for i in devices]
    return lax.ppermute(block, axis, route)


def on_device(
    queries, keys, values, frame_ids, past_keys, past_values, block_home, windows, window_len
):
    row_count = queries.shape[0]
    feature_width = queries.shape[1]
    head_count = feature_width // HEAD_DIM
    seq_count = lax.axis_size("seq")
    my_index = lax.axis_index("seq")
    score_scale = HEAD_DIM ** (-0.5)
    query_heads = queries.reshape(row_count, head_count, HEAD_DIM)

    def attend(carried, key_rows, value_rows, key_mask):
        run_max, run_sum, run_acc = carried
        scores = (
            jnp.einsum("qhd,khd->hqk", query_heads, key_rows, preferred_element_type=jnp.float32)
            * score_scale
        )
        scores = jnp.where(key_mask[None], scores, masked_score)
        new_max = jnp.maximum(run_max, jnp.max(scores, axis=-1))
        weights = jnp.where(key_mask[None], jnp.exp(scores - new_max[..., None]), 0.0)
        rescale = jnp.exp(run_max - new_max)
        run_sum = run_sum * rescale + jnp.sum(weights, axis=-1)
        update = jnp.einsum(
            "hqk,khd->qhd",
            weights.astype(jnp.bfloat16),
            value_rows,
            preferred_element_type=jnp.float32,
        )
        run_acc = run_acc * rescale.T[..., None] + update
        return (new_max, run_sum, run_acc)

    carried = (
        jnp.full((head_count, row_count), masked_score, jnp.float32),
        jnp.zeros((head_count, row_count), jnp.float32),
        jnp.zeros((row_count, head_count, HEAD_DIM), jnp.float32),
    )
    every_frame = lax.all_gather(frame_ids, "seq", axis=0, tiled=True)
    self_mask = frame_ids[None, :] <= frame_ids[:, None]
    carried = attend(
        carried,
        keys.reshape(row_count, head_count, HEAD_DIM),
        values.reshape(row_count, head_count, HEAD_DIM),
        self_mask,
    )

    def cycle_body(offset, loop_state):
        moving, running = loop_state
        moving = shifted(moving, "seq", 1)
        source = (my_index - offset) % seq_count
        key_frames = lax.dynamic_slice_in_dim(every_frame, source * row_count, row_count, 0)
        key_mask = key_frames[None, :] <= frame_ids[:, None]
        key_rows = moving[0].reshape(row_count, head_count, HEAD_DIM)
        value_rows = moving[1].reshape(row_count, head_count, HEAD_DIM)
        running = attend(running, key_rows, value_rows, key_mask)
        return (moving, running)

    moving = jnp.stack([keys, values])
    moving, carried = lax.fori_loop(1, seq_count, cycle_body, (moving, carried))
    list_len = windows.shape[1]
    block_len = past_keys.shape[1]
    my_rows = block_home[lax.dynamic_index_in_dim(windows, my_index, 0, keepdims=False)]
    my_len = lax.dynamic_index_in_dim(window_len, my_index, 0, keepdims=False)
    live_slots = jnp.arange(list_len) < my_len
    running = carried
    piece_keys = lax.all_gather(past_keys, "seq", axis=0, tiled=True)
    piece_values = lax.all_gather(past_values, "seq", axis=0, tiled=True)
    block_count = piece_keys.shape[0]
    grouping = math.gcd(block_count, 8)
    row_ids = jnp.arange(block_count)
    member = jnp.any((row_ids[:, None] == my_rows[None, :]) & live_slots[None, :], axis=1)
    group_keys = piece_keys.reshape(
        block_count // grouping, grouping * block_len, head_count, HEAD_DIM
    )
    group_values = piece_values.reshape(
        block_count // grouping, grouping * block_len, head_count, HEAD_DIM
    )
    group_mask = jnp.repeat(member.reshape(block_count // grouping, grouping), block_len, axis=1)

    def one_group(inside, items):
        item_keys, item_values, item_mask = items
        full_mask = jnp.broadcast_to(item_mask[None, :], (row_count, item_mask.shape[0]))
        return (attend(inside, item_keys, item_values, full_mask), None)

    running, unused = lax.scan(one_group, running, (group_keys, group_values, group_mask))
    carried = running
    run_max, run_sum, run_acc = carried
    output = run_acc / run_sum.T[..., None]
    return output.reshape(row_count, feature_width).astype(jnp.bfloat16)

MESH = pl.DeviceIdType.MESH
LOG2E = 1.4426950408889634


def dot_nt(a, b):
    return lax.dot_general(a, b, (((1,), (1,)), ((), ())), preferred_element_type=jnp.float32)


def dot_tn(a, b):
    return lax.dot_general(a, b, (((0,), (0,)), ((), ())), preferred_element_type=jnp.float32)


def heads_kernel(
    n,
    q_ref,
    k_ref,
    v_ref,
    frames_ref,
    pk_ref,
    pv_ref,
    home_ref,
    windows_ref,
    len_ref,
    out_ref,
    qb,
    kb,
    vb,
    fb,
    frame_col,
    pkb,
    pvb,
    past_k,
    past_v,
    ob,
    send_sem,
    recv_sem,
    own_sem,
    frame_send,
    frame_recv,
    out_send,
    out_recv,
    out_own,
):
    me = lax.axis_index("seq")
    rows = q_ref.shape[0]
    heads_here = qb.shape[0]
    width = heads_here * HEAD_DIM
    blocks = pk_ref.shape[0]
    blk = pk_ref.shape[1]
    win = windows_ref.shape[1]
    scale = LOG2E * HEAD_DIM ** (-0.5)

    barrier = pltpu.get_barrier_semaphore()
    for t in range(1, n):
        pl.semaphore_signal(
            barrier, inc=1, device_id={"seq": lax.rem(me + t, n)}, device_id_type=MESH
        )
    pl.semaphore_wait(barrier, n - 1)

    def pairs(h, dest, source):
        columns = pl.ds(pl.multiple_of(dest * width + h * HEAD_DIM, HEAD_DIM), HEAD_DIM)
        span = pl.ds(source * blocks, blocks)
        return [
            (q_ref.at[:, columns], qb.at[h, source]),
            (k_ref.at[:, columns], kb.at[h, source]),
            (v_ref.at[:, columns], vb.at[h, source]),
            (pk_ref.at[:, :, columns], pkb.at[h, span]),
            (pv_ref.at[:, :, columns], pvb.at[h, span]),
        ]

    def sends(h):
        made = []
        for t in range(1, n):
            dest = lax.rem(me + t, n)
            for i, (src, dst) in enumerate(pairs(h, dest, me)):
                made.append(
                    pltpu.make_async_remote_copy(
                        src_ref=src,
                        dst_ref=dst,
                        send_sem=send_sem.at[h, t, i],
                        recv_sem=recv_sem.at[h, t, i],
                        device_id={"seq": dest},
                        device_id_type=MESH,
                    )
                )
        return made

    def owns(h):
        return [
            pltpu.make_async_copy(src, dst, own_sem.at[h, i])
            for i, (src, dst) in enumerate(pairs(h, me, me))
        ]

    def frame_send_of(t):
        return pltpu.make_async_remote_copy(
            src_ref=frames_ref,
            dst_ref=fb.at[me],
            send_sem=frame_send.at[t],
            recv_sem=frame_recv.at[t],
            device_id={"seq": lax.rem(me + t, n)},
            device_id_type=MESH,
        )

    def start(h):
        for copy in sends(h):
            copy.start()
        for copy in owns(h):
            copy.start()

    for t in range(1, n):
        frame_send_of(t).start()
    start(0)
    if heads_here > 1:
        start(1)
    fb[me] = frames_ref[...]
    for t in range(1, n):
        frame_send_of(t).wait()
    for s in range(n):
        frame_col[s] = jnp.transpose(fb[s])

    def out_copy(h, t):
        dest = lax.rem(me + t, n)
        columns = pl.ds(pl.multiple_of(me * width + h * HEAD_DIM, HEAD_DIM), HEAD_DIM)
        return pltpu.make_async_remote_copy(
            src_ref=ob.at[h, dest],
            dst_ref=out_ref.at[:, columns],
            send_sem=out_send.at[h, t],
            recv_sem=out_recv.at[h, t],
            device_id={"seq": dest},
            device_id_type=MESH,
        )

    def out_own_copy(h):
        columns = pl.ds(pl.multiple_of(me * width + h * HEAD_DIM, HEAD_DIM), HEAD_DIM)
        return pltpu.make_async_copy(ob.at[h, me], out_ref.at[:, columns], out_own.at[h])

    def one_head(h, carry):
        for copy in sends(h):
            copy.wait_recv()
        for copy in owns(h):
            copy.wait()

        @pl.when(h + 2 < heads_here)
        def _():
            start(h + 2)

        past_k[...] = pkb[h]
        past_v[...] = pvb[h]
        for s in range(n):
            query = qb[h, s]
            state = (
                jnp.full((1, rows), -1e30, jnp.float32),
                jnp.zeros((1, rows), jnp.float32),
                jnp.zeros((HEAD_DIM, rows), jnp.float32),
            )

            def update(state, key, value, allowed):
                top, total, acc = state
                score = dot_nt(key, query) * scale
                if allowed is not None:
                    score = jnp.where(allowed, score, -1e30)
                new_top = jnp.maximum(top, jnp.max(score, axis=0, keepdims=True))
                weight = jnp.exp2(score - new_top)
                fade = jnp.exp2(top - new_top)
                total = total * fade + jnp.sum(weight, axis=0, keepdims=True)
                acc = acc * fade + dot_tn(value, weight.astype(jnp.bfloat16))
                return new_top, total, acc

            query_frame = fb[s, 0:1, :]
            for j in range(min(s + 2, n)):
                allowed = None
                if j >= s:
                    allowed = frame_col[j][:, 0:1] <= query_frame
                state = update(state, kb[h, j], vb[h, j], allowed)
            keys, values, live = [], [], []
            for w in range(win):
                row = home_ref[windows_ref[s, w]]
                keys.append(past_k[row])
                values.append(past_v[row])
            slot = lax.broadcasted_iota(jnp.int32, (win * blk, 1), 0) // blk
            live = slot < len_ref[s]
            top, total, acc = update(
                state, jnp.concatenate(keys, axis=0), jnp.concatenate(values, axis=0), live
            )
            ob[h, s] = jnp.transpose(acc / total).astype(jnp.bfloat16)
        for t in range(1, n):
            out_copy(h, t).start()
        out_own_copy(h).start()
        return carry

    lax.fori_loop(0, heads_here, one_head, 0)

    def finish(h, carry):
        for copy in sends(h):
            copy.wait_send()
        for t in range(1, n):
            out_copy(h, t).wait()
        out_own_copy(h).wait()
        return carry

    lax.fori_loop(0, heads_here, finish, 0)


def by_heads(
    queries, keys, values, frame_ids, past_keys, past_values, block_home, windows, window_len
):
    n = lax.axis_size("seq")
    rows, features = queries.shape
    heads_here = features // HEAD_DIM // n
    blocks, blk = past_keys.shape[0], past_keys.shape[1]
    frames = jnp.broadcast_to(frame_ids[None, :].astype(jnp.float32), (8, rows))
    anywhere = pl.BlockSpec(memory_space=pl.ANY)
    vmem = pl.BlockSpec(memory_space=pltpu.VMEM)
    smem = pl.BlockSpec(memory_space=pltpu.SMEM)
    dma = pltpu.SemaphoreType.DMA
    bf16 = jnp.bfloat16
    return pl.pallas_call(
        functools.partial(heads_kernel, n),
        out_shape=jax.ShapeDtypeStruct((rows, features), bf16),
        in_specs=[anywhere] * 3 + [vmem] + [anywhere] * 2 + [smem] * 3,
        out_specs=anywhere,
        scratch_shapes=[
            pltpu.VMEM((heads_here, n, rows, HEAD_DIM), bf16),
            pltpu.VMEM((heads_here, n, rows, HEAD_DIM), bf16),
            pltpu.VMEM((heads_here, n, rows, HEAD_DIM), bf16),
            pltpu.VMEM((n, 8, rows), jnp.float32),
            pltpu.VMEM((n, rows, 8), jnp.float32),
            pltpu.VMEM((heads_here, n * blocks, blk, HEAD_DIM), bf16),
            pltpu.VMEM((heads_here, n * blocks, blk, HEAD_DIM), bf16),
            pltpu.VMEM((n * blocks, blk, HEAD_DIM), bf16),
            pltpu.VMEM((n * blocks, blk, HEAD_DIM), bf16),
            pltpu.VMEM((heads_here, n, rows, HEAD_DIM), bf16),
            dma((heads_here, n, 5)),
            dma((heads_here, n, 5)),
            dma((heads_here, 5)),
            dma((n,)),
            dma((n,)),
            dma((heads_here, n)),
            dma((heads_here, n)),
            dma((heads_here,)),
        ],
        compiler_params=pltpu.CompilerParams(
            collective_id=0, has_side_effects=True, vmem_limit_bytes=48 * 1024 * 1024
        ),
    )(queries, keys, values, frames, past_keys, past_values, block_home, windows, window_len)


def pick(queries, *rest):
    heads = queries.shape[1] // HEAD_DIM
    if heads % lax.axis_size("seq") == 0:
        return by_heads(queries, *rest)
    return on_device(queries, *rest)


def solution(mesh):
    in_specs = (
        P(("clips", "seq"), ("cache", "head")),
        P(("clips", "seq"), ("cache", "head")),
        P(("clips", "seq"), ("cache", "head")),
        P(("clips", "seq")),
        P(("clips", "seq"), None, ("cache", "head")),
        P(("clips", "seq"), None, ("cache", "head")),
        P("clips"),
        P("clips", None),
        P("clips"),
    )
    out_specs = P(("clips", "seq"), ("cache", "head"))
    return jax.shard_map(
        pick, mesh=mesh, in_specs=in_specs, out_specs=out_specs, check_vma=False
    )
```

```python
import functools
import math

import jax
import jax.numpy as jnp
from jax import lax
from jax.experimental import pallas as pl
from jax.experimental.pallas import tpu as pltpu
from jax.sharding import PartitionSpec as P

HEAD_DIM = 128


masked_score = -1e30


def shifted(block, axis, distance):
    devices = range(lax.axis_size(axis))
    route = [((i - distance) % len(devices), i) for i in devices]
    return lax.ppermute(block, axis, route)


def on_device(
    queries, keys, values, frame_ids, past_keys, past_values, block_home, windows, window_len
):
    row_count = queries.shape[0]
    feature_width = queries.shape[1]
    head_count = feature_width // HEAD_DIM
    seq_count = lax.axis_size("seq")
    my_index = lax.axis_index("seq")
    score_scale = HEAD_DIM ** (-0.5)
    query_heads = queries.reshape(row_count, head_count, HEAD_DIM)

    def attend(carried, key_rows, value_rows, key_mask):
        run_max, run_sum, run_acc = carried
        scores = (
            jnp.einsum("qhd,khd->hqk", query_heads, key_rows, preferred_element_type=jnp.float32)
            * score_scale
        )
        scores = jnp.where(key_mask[None], scores, masked_score)
        new_max = jnp.maximum(run_max, jnp.max(scores, axis=-1))
        weights = jnp.where(key_mask[None], jnp.exp(scores - new_max[..., None]), 0.0)
        rescale = jnp.exp(run_max - new_max)
        run_sum = run_sum * rescale + jnp.sum(weights, axis=-1)
        update = jnp.einsum(
            "hqk,khd->qhd",
            weights.astype(jnp.bfloat16),
            value_rows,
            preferred_element_type=jnp.float32,
        )
        run_acc = run_acc * rescale.T[..., None] + update
        return (new_max, run_sum, run_acc)

    carried = (
        jnp.full((head_count, row_count), masked_score, jnp.float32),
        jnp.zeros((head_count, row_count), jnp.float32),
        jnp.zeros((row_count, head_count, HEAD_DIM), jnp.float32),
    )
    every_frame = lax.all_gather(frame_ids, "seq", axis=0, tiled=True)
    self_mask = frame_ids[None, :] <= frame_ids[:, None]
    carried = attend(
        carried,
        keys.reshape(row_count, head_count, HEAD_DIM),
        values.reshape(row_count, head_count, HEAD_DIM),
        self_mask,
    )

    def cycle_body(offset, loop_state):
        moving, running = loop_state
        moving = shifted(moving, "seq", 1)
        source = (my_index - offset) % seq_count
        key_frames = lax.dynamic_slice_in_dim(every_frame, source * row_count, row_count, 0)
        key_mask = key_frames[None, :] <= frame_ids[:, None]
        key_rows = moving[0].reshape(row_count, head_count, HEAD_DIM)
        value_rows = moving[1].reshape(row_count, head_count, HEAD_DIM)
        running = attend(running, key_rows, value_rows, key_mask)
        return (moving, running)

    moving = jnp.stack([keys, values])
    moving, carried = lax.fori_loop(1, seq_count, cycle_body, (moving, carried))
    list_len = windows.shape[1]
    block_len = past_keys.shape[1]
    my_rows = block_home[lax.dynamic_index_in_dim(windows, my_index, 0, keepdims=False)]
    my_len = lax.dynamic_index_in_dim(window_len, my_index, 0, keepdims=False)
    live_slots = jnp.arange(list_len) < my_len
    running = carried
    piece_keys = lax.all_gather(past_keys, "seq", axis=0, tiled=True)
    piece_values = lax.all_gather(past_values, "seq", axis=0, tiled=True)
    block_count = piece_keys.shape[0]
    grouping = math.gcd(block_count, 8)
    row_ids = jnp.arange(block_count)
    member = jnp.any((row_ids[:, None] == my_rows[None, :]) & live_slots[None, :], axis=1)
    group_keys = piece_keys.reshape(
        block_count // grouping, grouping * block_len, head_count, HEAD_DIM
    )
    group_values = piece_values.reshape(
        block_count // grouping, grouping * block_len, head_count, HEAD_DIM
    )
    group_mask = jnp.repeat(member.reshape(block_count // grouping, grouping), block_len, axis=1)

    def one_group(inside, items):
        item_keys, item_values, item_mask = items
        full_mask = jnp.broadcast_to(item_mask[None, :], (row_count, item_mask.shape[0]))
        return (attend(inside, item_keys, item_values, full_mask), None)

    running, unused = lax.scan(one_group, running, (group_keys, group_values, group_mask))
    carried = running
    run_max, run_sum, run_acc = carried
    output = run_acc / run_sum.T[..., None]
    return output.reshape(row_count, feature_width).astype(jnp.bfloat16)

MESH = pl.DeviceIdType.MESH
LOG2E = 1.4426950408889634


def dot_nt(a, b):
    return lax.dot_general(a, b, (((1,), (1,)), ((), ())), preferred_element_type=jnp.float32)


def dot_tn(a, b):
    return lax.dot_general(a, b, (((0,), (0,)), ((), ())), preferred_element_type=jnp.float32)


def heads_kernel(
    q_ref,
    k_ref,
    v_ref,
    frames_ref,
    pk_ref,
    pv_ref,
    home_ref,
    windows_ref,
    len_ref,
    out_ref,
    qb,
    kb,
    vb,
    fb,
    frame_col,
    pkb,
    pvb,
    past_k,
    past_v,
    part,
    part_lse,
    got,
    got_lse,
    own_acc,
    own_stat,
    ob,
    q_send,
    q_recv,
    kv_send,
    kv_recv,
    own_sem,
    frame_send,
    frame_recv,
    part_send,
    part_recv,
    out_send,
    out_recv,
    out_own,
):
    n = 4
    me = lax.axis_index("seq")
    side = lax.rem(me, 2)
    half = me // 2
    mate = me + 1 - 2 * side
    peer = lax.rem(me + 2, n)
    rows = q_ref.shape[0]
    heads_here = qb.shape[0]
    width = heads_here * HEAD_DIM
    blocks = pk_ref.shape[0]
    blk = pk_ref.shape[1]
    win = windows_ref.shape[1]
    scale = LOG2E * HEAD_DIM ** (-0.5)

    barrier = pltpu.get_barrier_semaphore()
    for t in range(1, n):
        pl.semaphore_signal(
            barrier, inc=1, device_id={"seq": lax.rem(me + t, n)}, device_id_type=MESH
        )
    pl.semaphore_wait(barrier, n - 1)

    def head_columns(which, h):
        return pl.ds(pl.multiple_of(which * width + h * HEAD_DIM, HEAD_DIM), HEAD_DIM)

    def remote(src, dst, send, recv, dest):
        return pltpu.make_async_remote_copy(
            src_ref=src,
            dst_ref=dst,
            send_sem=send,
            recv_sem=recv,
            device_id={"seq": dest},
            device_id_type=MESH,
        )

    def stationary(h, which):
        columns = head_columns(which, h)
        span = pl.ds(side * blocks, blocks)
        return [
            (k_ref.at[:, columns], kb.at[h, side]),
            (v_ref.at[:, columns], vb.at[h, side]),
            (pk_ref.at[:, :, columns], pkb.at[h, span]),
            (pv_ref.at[:, :, columns], pvb.at[h, span]),
        ]

    def sends(h):
        made = [
            remote(src, dst, kv_send.at[h, i], kv_recv.at[h, i], mate)
            for i, (src, dst) in enumerate(stationary(h, 1 - side))
        ]
        for t in range(1, n):
            dest = lax.rem(me + t, n)
            columns = head_columns(lax.rem(dest, 2), h)
            made.append(
                remote(q_ref.at[:, columns], qb.at[h, me], q_send.at[h, t], q_recv.at[h, t], dest)
            )
        return made

    def owns(h):
        mine = stationary(h, side) + [(q_ref.at[:, head_columns(side, h)], qb.at[h, me])]
        return [
            pltpu.make_async_copy(src, dst, own_sem.at[h, i]) for i, (src, dst) in enumerate(mine)
        ]

    def frame_send_of(t):
        return remote(
            frames_ref, fb.at[me], frame_send.at[t], frame_recv.at[t], lax.rem(me + t, n)
        )

    def start(h):
        for copy in sends(h):
            copy.start()
        for copy in owns(h):
            copy.start()

    def part_copies(h):
        return [
            remote(part.at[h], got.at[h], part_send.at[h, 0], part_recv.at[h, 0], peer),
            remote(part_lse.at[h], got_lse.at[h], part_send.at[h, 1], part_recv.at[h, 1], peer),
        ]

    def out_copy(h):
        return remote(
            ob.at[h, 1 - side],
            out_ref.at[:, head_columns(side, h)],
            out_send.at[h],
            out_recv.at[h],
            mate,
        )

    def out_own_copy(h):
        return pltpu.make_async_copy(
            ob.at[h, side], out_ref.at[:, head_columns(side, h)], out_own.at[h]
        )

    for t in range(1, n):
        frame_send_of(t).start()
    start(0)
    start(1)
    fb[me] = frames_ref[...]
    for t in range(1, n):
        frame_send_of(t).wait()
    for s in range(n):
        frame_col[s] = jnp.transpose(fb[s])

    def attend(h, g, s):
        query = qb[h, s]
        state = (
            jnp.full((1, rows), -1e30, jnp.float32),
            jnp.zeros((1, rows), jnp.float32),
            jnp.zeros((HEAD_DIM, rows), jnp.float32),
        )

        def update(state, key, value, allowed):
            top, total, acc = state
            score = dot_nt(key, query) * scale
            if allowed is not None:
                score = jnp.where(allowed, score, -1e30)
            new_top = jnp.maximum(top, jnp.max(score, axis=0, keepdims=True))
            weight = jnp.exp2(score - new_top)
            fade = jnp.exp2(top - new_top)
            total = total * fade + jnp.sum(weight, axis=0, keepdims=True)
            acc = acc * fade + dot_tn(value, weight.astype(jnp.bfloat16))
            return new_top, total, acc

        query_frame = fb[s, 0:1, :]
        for i in range(2):
            j = 2 * g + i
            if j <= s + 1:
                allowed = frame_col[j][:, 0:1] <= query_frame if j >= s else None
                state = update(state, kb[h, i], vb[h, i], allowed)
        keys, values = [], []
        slot = lax.broadcasted_iota(jnp.int32, (win * blk, 1), 0) // blk
        live = jnp.zeros((win * blk, 1), jnp.int32)
        for w in range(win):
            row = home_ref[windows_ref[s, w]]
            keys.append(past_k[lax.rem(row, 2 * blocks)])
            values.append(past_v[lax.rem(row, 2 * blocks)])
            here = (row // (2 * blocks) == g) & (w < len_ref[s])
            live = jnp.where(slot == w, here.astype(jnp.int32), live)
        return update(
            state, jnp.concatenate(keys, axis=0), jnp.concatenate(values, axis=0), live > 0
        )

    def merge(h):
        for copy in part_copies(h):
            copy.wait_recv()
        for k in range(2):
            top, total = own_stat[h, k, 0:1], own_stat[h, k, 1:2]
            other = got_lse[h, k : k + 1]
            new_top = jnp.maximum(top, other)
            mine, theirs = jnp.exp2(top - new_top), jnp.exp2(other - new_top)
            mixed = own_acc[h, k] * mine + got[h, k].astype(jnp.float32) * theirs
            ob[h, k] = jnp.transpose(mixed / (total * mine + theirs)).astype(jnp.bfloat16)
        out_copy(h).start()
        out_own_copy(h).start()

    def one_head(h, carry):
        for copy in sends(h):
            copy.wait_recv()
        for copy in owns(h):
            copy.wait()

        @pl.when(h + 2 < heads_here)
        def _():
            start(h + 2)

        past_k[...] = pkb[h]
        past_v[...] = pvb[h]

        def away(g):
            for k in range(2):
                top, total, acc = attend(h, g, 2 * (1 - g) + k)
                part[h, k] = (acc / total).astype(jnp.bfloat16)
                part_lse[h, k : k + 1] = top + jnp.log2(total)

        def home(g):
            for k in range(2):
                top, total, acc = attend(h, g, 2 * g + k)
                own_acc[h, k] = acc
                own_stat[h, k, 0:1] = top
                own_stat[h, k, 1:2] = total

        for g in range(2):
            pl.when(half == g)(functools.partial(away, g))
        for copy in part_copies(h):
            copy.start()
        for g in range(2):
            pl.when(half == g)(functools.partial(home, g))

        @pl.when(h > 0)
        def _():
            merge(h - 1)

        return carry

    lax.fori_loop(0, heads_here, one_head, 0)
    merge(heads_here - 1)

    def finish(h, carry):
        for copy in sends(h):
            copy.wait_send()
        for copy in part_copies(h):
            copy.wait_send()
        out_copy(h).wait()
        out_own_copy(h).wait()
        return carry

    lax.fori_loop(0, heads_here, finish, 0)


def by_heads(
    queries, keys, values, frame_ids, past_keys, past_values, block_home, windows, window_len
):
    n = lax.axis_size("seq")
    rows, features = queries.shape
    heads_here = features // HEAD_DIM // 2
    blocks, blk = past_keys.shape[0], past_keys.shape[1]
    frames = jnp.broadcast_to(frame_ids[None, :].astype(jnp.float32), (8, rows))
    anywhere = pl.BlockSpec(memory_space=pl.ANY)
    vmem = pl.BlockSpec(memory_space=pltpu.VMEM)
    smem = pl.BlockSpec(memory_space=pltpu.SMEM)
    dma = pltpu.SemaphoreType.DMA
    bf16, f32 = jnp.bfloat16, jnp.float32
    return pl.pallas_call(
        heads_kernel,
        out_shape=jax.ShapeDtypeStruct((rows, features), bf16),
        in_specs=[anywhere] * 3 + [vmem] + [anywhere] * 2 + [smem] * 3,
        out_specs=anywhere,
        scratch_shapes=[
            pltpu.VMEM((heads_here, n, rows, HEAD_DIM), bf16),
            pltpu.VMEM((heads_here, 2, rows, HEAD_DIM), bf16),
            pltpu.VMEM((heads_here, 2, rows, HEAD_DIM), bf16),
            pltpu.VMEM((n, 8, rows), f32),
            pltpu.VMEM((n, rows, 8), f32),
            pltpu.VMEM((heads_here, 2 * blocks, blk, HEAD_DIM), bf16),
            pltpu.VMEM((heads_here, 2 * blocks, blk, HEAD_DIM), bf16),
            pltpu.VMEM((2 * blocks, blk, HEAD_DIM), bf16),
            pltpu.VMEM((2 * blocks, blk, HEAD_DIM), bf16),
            pltpu.VMEM((heads_here, 2, HEAD_DIM, rows), bf16),
            pltpu.VMEM((heads_here, 2, rows), f32),
            pltpu.VMEM((heads_here, 2, HEAD_DIM, rows), bf16),
            pltpu.VMEM((heads_here, 2, rows), f32),
            pltpu.VMEM((heads_here, 2, HEAD_DIM, rows), f32),
            pltpu.VMEM((heads_here, 2, 2, rows), f32),
            pltpu.VMEM((heads_here, 2, rows, HEAD_DIM), bf16),
            dma((heads_here, n)),
            dma((heads_here, n)),
            dma((heads_here, 4)),
            dma((heads_here, 4)),
            dma((heads_here, 5)),
            dma((n,)),
            dma((n,)),
            dma((heads_here, 2)),
            dma((heads_here, 2)),
            dma((heads_here,)),
            dma((heads_here,)),
            dma((heads_here,)),
        ],
        compiler_params=pltpu.CompilerParams(
            collective_id=0, has_side_effects=True, vmem_limit_bytes=48 * 1024 * 1024
        ),
    )(queries, keys, values, frames, past_keys, past_values, block_home, windows, window_len)


def pick(queries, *rest):
    heads = queries.shape[1] // HEAD_DIM
    if lax.axis_size("seq") == 4 and heads % 2 == 0 and heads >= 4:
        return by_heads(queries, *rest)
    return on_device(queries, *rest)


def solution(mesh):
    in_specs = (
        P(("clips", "seq"), ("cache", "head")),
        P(("clips", "seq"), ("cache", "head")),
        P(("clips", "seq"), ("cache", "head")),
        P(("clips", "seq")),
        P(("clips", "seq"), None, ("cache", "head")),
        P(("clips", "seq"), None, ("cache", "head")),
        P("clips"),
        P("clips", None),
        P("clips"),
    )
    out_specs = P(("clips", "seq"), ("cache", "head"))
    return jax.shard_map(
        pick, mesh=mesh, in_specs=in_specs, out_specs=out_specs, check_vma=False
    )
```

```python
import functools
import math

import jax
import jax.numpy as jnp
from jax import lax
from jax.experimental import pallas as pl
from jax.experimental.pallas import tpu as pltpu
from jax.sharding import PartitionSpec as P

HEAD_DIM = 128


masked_score = -1e30


def shifted(block, axis, distance):
    devices = range(lax.axis_size(axis))
    route = [((i - distance) % len(devices), i) for i in devices]
    return lax.ppermute(block, axis, route)


def on_device(
    queries, keys, values, frame_ids, past_keys, past_values, block_home, windows, window_len
):
    row_count = queries.shape[0]
    feature_width = queries.shape[1]
    head_count = feature_width // HEAD_DIM
    seq_count = lax.axis_size("seq")
    my_index = lax.axis_index("seq")
    score_scale = HEAD_DIM ** (-0.5)
    query_heads = queries.reshape(row_count, head_count, HEAD_DIM)

    def attend(carried, key_rows, value_rows, key_mask):
        run_max, run_sum, run_acc = carried
        scores = (
            jnp.einsum("qhd,khd->hqk", query_heads, key_rows, preferred_element_type=jnp.float32)
            * score_scale
        )
        scores = jnp.where(key_mask[None], scores, masked_score)
        new_max = jnp.maximum(run_max, jnp.max(scores, axis=-1))
        weights = jnp.where(key_mask[None], jnp.exp(scores - new_max[..., None]), 0.0)
        rescale = jnp.exp(run_max - new_max)
        run_sum = run_sum * rescale + jnp.sum(weights, axis=-1)
        update = jnp.einsum(
            "hqk,khd->qhd",
            weights.astype(jnp.bfloat16),
            value_rows,
            preferred_element_type=jnp.float32,
        )
        run_acc = run_acc * rescale.T[..., None] + update
        return (new_max, run_sum, run_acc)

    carried = (
        jnp.full((head_count, row_count), masked_score, jnp.float32),
        jnp.zeros((head_count, row_count), jnp.float32),
        jnp.zeros((row_count, head_count, HEAD_DIM), jnp.float32),
    )
    every_frame = lax.all_gather(frame_ids, "seq", axis=0, tiled=True)
    self_mask = frame_ids[None, :] <= frame_ids[:, None]
    carried = attend(
        carried,
        keys.reshape(row_count, head_count, HEAD_DIM),
        values.reshape(row_count, head_count, HEAD_DIM),
        self_mask,
    )

    def cycle_body(offset, loop_state):
        moving, running = loop_state
        moving = shifted(moving, "seq", 1)
        source = (my_index - offset) % seq_count
        key_frames = lax.dynamic_slice_in_dim(every_frame, source * row_count, row_count, 0)
        key_mask = key_frames[None, :] <= frame_ids[:, None]
        key_rows = moving[0].reshape(row_count, head_count, HEAD_DIM)
        value_rows = moving[1].reshape(row_count, head_count, HEAD_DIM)
        running = attend(running, key_rows, value_rows, key_mask)
        return (moving, running)

    moving = jnp.stack([keys, values])
    moving, carried = lax.fori_loop(1, seq_count, cycle_body, (moving, carried))
    list_len = windows.shape[1]
    block_len = past_keys.shape[1]
    my_rows = block_home[lax.dynamic_index_in_dim(windows, my_index, 0, keepdims=False)]
    my_len = lax.dynamic_index_in_dim(window_len, my_index, 0, keepdims=False)
    live_slots = jnp.arange(list_len) < my_len
    running = carried
    piece_keys = lax.all_gather(past_keys, "seq", axis=0, tiled=True)
    piece_values = lax.all_gather(past_values, "seq", axis=0, tiled=True)
    block_count = piece_keys.shape[0]
    grouping = math.gcd(block_count, 8)
    row_ids = jnp.arange(block_count)
    member = jnp.any((row_ids[:, None] == my_rows[None, :]) & live_slots[None, :], axis=1)
    group_keys = piece_keys.reshape(
        block_count // grouping, grouping * block_len, head_count, HEAD_DIM
    )
    group_values = piece_values.reshape(
        block_count // grouping, grouping * block_len, head_count, HEAD_DIM
    )
    group_mask = jnp.repeat(member.reshape(block_count // grouping, grouping), block_len, axis=1)

    def one_group(inside, items):
        item_keys, item_values, item_mask = items
        full_mask = jnp.broadcast_to(item_mask[None, :], (row_count, item_mask.shape[0]))
        return (attend(inside, item_keys, item_values, full_mask), None)

    running, unused = lax.scan(one_group, running, (group_keys, group_values, group_mask))
    carried = running
    run_max, run_sum, run_acc = carried
    output = run_acc / run_sum.T[..., None]
    return output.reshape(row_count, feature_width).astype(jnp.bfloat16)

MESH = pl.DeviceIdType.MESH
LOG2E = 1.4426950408889634


def dot_nt(a, b):
    return lax.dot_general(a, b, (((1,), (1,)), ((), ())), preferred_element_type=jnp.float32)


def dot_tn(a, b):
    return lax.dot_general(a, b, (((0,), (0,)), ((), ())), preferred_element_type=jnp.float32)


def heads_kernel(
    q_ref,
    k_ref,
    v_ref,
    frames_ref,
    pk_ref,
    pv_ref,
    home_ref,
    windows_ref,
    len_ref,
    out_ref,
    qb,
    kb,
    vb,
    fb,
    frame_col,
    pkb,
    pvb,
    past_k,
    past_v,
    part,
    part_lse,
    got,
    got_lse,
    met,
    met_lse,
    own_acc,
    own_stat,
    ob,
    ob_met,
    q_send,
    q_recv,
    relay_send,
    kv_send,
    kv_recv,
    own_sem,
    frame_send,
    frame_recv,
    part_send,
    part_recv,
    out_send,
    out_recv,
    out_own,
    out_met,
):
    n = 4
    me = lax.axis_index("seq")
    side = lax.rem(me, 2)
    half = me // 2
    mate = me + 1 - 2 * side
    peer = lax.rem(me + 2, n)
    outer = side == half
    inner = side != half
    rows = q_ref.shape[0]
    heads_here = qb.shape[0]
    width = heads_here * HEAD_DIM
    blocks = pk_ref.shape[0]
    blk = pk_ref.shape[1]
    win = windows_ref.shape[1]
    scale = LOG2E * HEAD_DIM ** (-0.5)

    barrier = pltpu.get_barrier_semaphore()
    for t in range(1, n):
        pl.semaphore_signal(
            barrier, inc=1, device_id={"seq": lax.rem(me + t, n)}, device_id_type=MESH
        )
    pl.semaphore_wait(barrier, n - 1)

    def head_columns(which, h):
        return pl.ds(pl.multiple_of(which * width + h * HEAD_DIM, HEAD_DIM), HEAD_DIM)

    def remote(src, dst, send, recv, dest):
        return pltpu.make_async_remote_copy(
            src_ref=src,
            dst_ref=dst,
            send_sem=send,
            recv_sem=recv,
            device_id={"seq": dest},
            device_id_type=MESH,
        )

    def stationary(h, which):
        columns = head_columns(which, h)
        span = pl.ds(side * blocks, blocks)
        return [
            (k_ref.at[:, columns], kb.at[h, side]),
            (v_ref.at[:, columns], vb.at[h, side]),
            (pk_ref.at[:, :, columns], pkb.at[h, span]),
            (pv_ref.at[:, :, columns], pvb.at[h, span]),
        ]

    def kv_sends(h):
        return [
            remote(src, dst, kv_send.at[h, i], kv_recv.at[h, i], mate)
            for i, (src, dst) in enumerate(stationary(h, 1 - side))
        ]

    def q_copy(h, t):
        dest = lax.rem(me + t, n)
        columns = head_columns(lax.rem(dest, 2), h)
        return remote(q_ref.at[:, columns], qb.at[h, me], q_send.at[h, t], q_recv.at[h, t], dest)

    def direct(t):
        return jnp.logical_or(inner, lax.rem(me + t, n) != n - 1 - me)

    def unrelayed(t):
        return jnp.logical_or(outer, lax.rem(me - t + n, n) != mate)

    def relay_copy(h):
        dest = n - 1 - mate
        t = lax.rem(dest - mate + n, n)
        return remote(qb.at[h, mate], qb.at[h, mate], relay_send.at[h], q_recv.at[h, t], dest)

    def relay(h):
        @pl.when(inner)
        def _():
            q_copy(h, lax.rem(me - mate + n, n)).wait_recv()
            relay_copy(h).start()

    def owns(h):
        mine = stationary(h, side) + [(q_ref.at[:, head_columns(side, h)], qb.at[h, me])]
        return [
            pltpu.make_async_copy(src, dst, own_sem.at[h, i]) for i, (src, dst) in enumerate(mine)
        ]

    def frame_send_of(t):
        return remote(
            frames_ref, fb.at[me], frame_send.at[t], frame_recv.at[t], lax.rem(me + t, n)
        )

    def start(h):
        for t in (1, 3, 2):
            pl.when(direct(t))(q_copy(h, t).start)
        for copy in kv_sends(h):
            copy.start()
        for copy in owns(h):
            copy.start()

    def both(h, i, src, dst, dst_lse, where, dest):
        return [
            remote(part.at[h, src], dst.at[h, where], part_send.at[h, i, 0], part_recv.at[h, i, 0], dest),
            remote(part_lse.at[h, src], dst_lse.at[h, where], part_send.at[h, i, 1], part_recv.at[h, i, 1], dest),
        ]

    def far_outer(h):
        return both(h, 0, 1 - half, got, got_lse, 1 - half, peer)

    def far_inner_by_outer(h):
        return both(h, 1, half, got, got_lse, half, peer)

    def far_inner_by_inner(h):
        return both(h, 2, half, met, met_lse, 1, n - 1 - me)

    def near_inner_by_outer(h):
        return both(h, 3, 2, met, met_lse, 0, mate)

    def out_copy(h):
        return remote(
            ob.at[h, 1 - side],
            out_ref.at[:, head_columns(side, h)],
            out_send.at[h],
            out_recv.at[h],
            mate,
        )

    def out_own_copy(h):
        return pltpu.make_async_copy(
            ob.at[h, side], out_ref.at[:, head_columns(side, h)], out_own.at[h]
        )

    def out_met_copy(h):
        return pltpu.make_async_copy(
            ob_met.at[h], out_ref.at[:, head_columns(1 - side, h)], out_met.at[h]
        )

    for t in range(1, n):
        frame_send_of(t).start()
    start(0)
    start(1)
    start(2)
    fb[me] = frames_ref[...]
    for t in range(1, n):
        frame_send_of(t).wait()
    for s in range(n):
        frame_col[s] = jnp.transpose(fb[s])
    relay(0)

    def attend(h, g, s):
        query = qb[h, s]
        state = (
            jnp.full((1, rows), -1e30, jnp.float32),
            jnp.zeros((1, rows), jnp.float32),
            jnp.zeros((HEAD_DIM, rows), jnp.float32),
        )

        def update(state, key, value, allowed):
            top, total, acc = state
            score = dot_nt(key, query) * scale
            if allowed is not None:
                score = jnp.where(allowed, score, -1e30)
            new_top = jnp.maximum(top, jnp.max(score, axis=0, keepdims=True))
            weight = jnp.exp2(score - new_top)
            fade = jnp.exp2(top - new_top)
            total = total * fade + jnp.sum(weight, axis=0, keepdims=True)
            acc = acc * fade + dot_tn(value, weight.astype(jnp.bfloat16))
            return new_top, total, acc

        query_frame = fb[s, 0:1, :]
        for i in range(2):
            j = 2 * g + i
            if j <= s + 1:
                allowed = frame_col[j][:, 0:1] <= query_frame if j >= s else None
                state = update(state, kb[h, i], vb[h, i], allowed)
        keys, values = [], []
        slot = lax.broadcasted_iota(jnp.int32, (win * blk, 1), 0) // blk
        live = jnp.zeros((win * blk, 1), jnp.int32)
        for w in range(win):
            row = home_ref[windows_ref[s, w]]
            keys.append(past_k[lax.rem(row, 2 * blocks)])
            values.append(past_v[lax.rem(row, 2 * blocks)])
            here = (row // (2 * blocks) == g) & (w < len_ref[s])
            live = jnp.where(slot == w, here.astype(jnp.int32), live)
        return update(
            state, jnp.concatenate(keys, axis=0), jnp.concatenate(values, axis=0), live > 0
        )

    def merge_own(h, k):
        top, total = own_stat[h, k, 0:1], own_stat[h, k, 1:2]
        other = got_lse[h, k]
        new_top = jnp.maximum(top, other)
        mine, theirs = jnp.exp2(top - new_top), jnp.exp2(other - new_top)
        mixed = own_acc[h, k] * mine + got[h, k].astype(jnp.float32) * theirs
        ob[h, k] = jnp.transpose(mixed / (total * mine + theirs)).astype(jnp.bfloat16)

    def merge_met(h):
        one, two = met_lse[h, 0], met_lse[h, 1]
        top = jnp.maximum(one, two)
        one, two = jnp.exp2(one - top), jnp.exp2(two - top)
        mixed = met[h, 0].astype(jnp.float32) * one + met[h, 1].astype(jnp.float32) * two
        ob_met[h] = jnp.transpose(mixed / (one + two)).astype(jnp.bfloat16)

    def merge(h):
        for copy in both(h, 0, 0, got, got_lse, half, peer):
            copy.wait_recv()
        merge_own(h, half)

        @pl.when(outer)
        def _():
            out_own_copy(h).start()

        @pl.when(inner)
        def _():
            out_copy(h).start()
            for copy in both(h, 1, 0, got, got_lse, 1 - half, peer):
                copy.wait_recv()
            merge_own(h, 1 - half)
            out_own_copy(h).start()
            for copy in far_inner_by_inner(h) + near_inner_by_outer(h):
                copy.wait_recv()
            merge_met(h)
            out_met_copy(h).start()

    def one_head(h, carry):
        for t in range(1, n):
            pl.when(unrelayed(t))(q_copy(h, t).wait_recv)
        for copy in kv_sends(h):
            copy.wait_recv()
        for copy in owns(h):
            copy.wait()

        @pl.when(h + 3 < heads_here)
        def _():
            start(h + 3)

        past_k[...] = pkb[h]
        past_v[...] = pvb[h]

        def away(g):
            for k in range(2):
                top, total, acc = attend(h, g, 2 * (1 - g) + k)
                part[h, k] = (acc / total).astype(jnp.bfloat16)
                part_lse[h, k] = top + jnp.log2(total)

        def home(g):
            for k in range(2):
                top, total, acc = attend(h, g, 2 * g + k)
                own_acc[h, k] = acc
                own_stat[h, k, 0:1] = top
                own_stat[h, k, 1:2] = total
                if k != g:
                    part[h, 2] = (acc / total).astype(jnp.bfloat16)
                    part_lse[h, 2] = top + jnp.log2(total)

        for g in range(2):
            pl.when(half == g)(functools.partial(away, g))
        for copy in far_outer(h):
            copy.start()

        @pl.when(outer)
        def _():
            for copy in far_inner_by_outer(h):
                copy.start()

        @pl.when(inner)
        def _():
            for copy in far_inner_by_inner(h):
                copy.start()

        @pl.when(h + 1 < heads_here)
        def _():
            relay(h + 1)

        for g in range(2):
            pl.when(half == g)(functools.partial(home, g))

        @pl.when(outer)
        def _():
            for copy in near_inner_by_outer(h):
                copy.start()

        @pl.when(h > 0)
        def _():
            merge(h - 1)

        return carry

    lax.fori_loop(0, heads_here, one_head, 0)
    merge(heads_here - 1)

    def finish(h, carry):
        for t in range(1, n):
            pl.when(direct(t))(q_copy(h, t).wait_send)
        for copy in kv_sends(h) + far_outer(h):
            copy.wait_send()
        out_own_copy(h).wait()

        @pl.when(outer)
        def _():
            for copy in far_inner_by_outer(h) + near_inner_by_outer(h):
                copy.wait_send()
            out_copy(h).wait_recv()

        @pl.when(inner)
        def _():
            relay_copy(h).wait_send()
            for copy in far_inner_by_inner(h):
                copy.wait_send()
            out_copy(h).wait_send()
            out_met_copy(h).wait()

        return carry

    lax.fori_loop(0, heads_here, finish, 0)


def by_heads(
    queries, keys, values, frame_ids, past_keys, past_values, block_home, windows, window_len
):
    n = lax.axis_size("seq")
    rows, features = queries.shape
    heads_here = features // HEAD_DIM // 2
    blocks, blk = past_keys.shape[0], past_keys.shape[1]
    frames = jnp.broadcast_to(frame_ids[None, :].astype(jnp.float32), (8, rows))
    anywhere = pl.BlockSpec(memory_space=pl.ANY)
    vmem = pl.BlockSpec(memory_space=pltpu.VMEM)
    smem = pl.BlockSpec(memory_space=pltpu.SMEM)
    dma = pltpu.SemaphoreType.DMA
    bf16, f32 = jnp.bfloat16, jnp.float32
    return pl.pallas_call(
        heads_kernel,
        out_shape=jax.ShapeDtypeStruct((rows, features), bf16),
        in_specs=[anywhere] * 3 + [vmem] + [anywhere] * 2 + [smem] * 3,
        out_specs=anywhere,
        scratch_shapes=[
            pltpu.VMEM((heads_here, n, rows, HEAD_DIM), bf16),
            pltpu.VMEM((heads_here, 2, rows, HEAD_DIM), bf16),
            pltpu.VMEM((heads_here, 2, rows, HEAD_DIM), bf16),
            pltpu.VMEM((n, 8, rows), f32),
            pltpu.VMEM((n, rows, 8), f32),
            pltpu.VMEM((heads_here, 2 * blocks, blk, HEAD_DIM), bf16),
            pltpu.VMEM((heads_here, 2 * blocks, blk, HEAD_DIM), bf16),
            pltpu.VMEM((2 * blocks, blk, HEAD_DIM), bf16),
            pltpu.VMEM((2 * blocks, blk, HEAD_DIM), bf16),
            pltpu.VMEM((heads_here, 3, HEAD_DIM, rows), bf16),
            pltpu.VMEM((heads_here, 3, 1, rows), f32),
            pltpu.VMEM((heads_here, 2, HEAD_DIM, rows), bf16),
            pltpu.VMEM((heads_here, 2, 1, rows), f32),
            pltpu.VMEM((heads_here, 2, HEAD_DIM, rows), bf16),
            pltpu.VMEM((heads_here, 2, 1, rows), f32),
            pltpu.VMEM((heads_here, 2, HEAD_DIM, rows), f32),
            pltpu.VMEM((heads_here, 2, 2, rows), f32),
            pltpu.VMEM((heads_here, 2, rows, HEAD_DIM), bf16),
            pltpu.VMEM((heads_here, rows, HEAD_DIM), bf16),
            dma((heads_here, n)),
            dma((heads_here, n)),
            dma((heads_here,)),
            dma((heads_here, 4)),
            dma((heads_here, 4)),
            dma((heads_here, 5)),
            dma((n,)),
            dma((n,)),
            dma((heads_here, 4, 2)),
            dma((heads_here, 4, 2)),
            dma((heads_here,)),
            dma((heads_here,)),
            dma((heads_here,)),
            dma((heads_here,)),
        ],
        compiler_params=pltpu.CompilerParams(
            collective_id=0, has_side_effects=True, vmem_limit_bytes=48 * 1024 * 1024
        ),
    )(queries, keys, values, frames, past_keys, past_values, block_home, windows, window_len)


def pick(queries, *rest):
    heads = queries.shape[1] // HEAD_DIM
    if lax.axis_size("seq") == 4 and heads % 2 == 0 and heads >= 6:
        return by_heads(queries, *rest)
    return on_device(queries, *rest)


def solution(mesh):
    in_specs = (
        P(("clips", "seq"), ("cache", "head")),
        P(("clips", "seq"), ("cache", "head")),
        P(("clips", "seq"), ("cache", "head")),
        P(("clips", "seq")),
        P(("clips", "seq"), None, ("cache", "head")),
        P(("clips", "seq"), None, ("cache", "head")),
        P("clips"),
        P("clips", None),
        P("clips"),
    )
    out_specs = P(("clips", "seq"), ("cache", "head"))
    return jax.shard_map(
        pick, mesh=mesh, in_specs=in_specs, out_specs=out_specs, check_vma=False
    )
```

```python
import functools
import math

import jax
import jax.numpy as jnp
from jax import lax
from jax.experimental import pallas as pl
from jax.experimental.pallas import tpu as pltpu
from jax.sharding import PartitionSpec as P

HEAD_DIM = 128


masked_score = -1e30


def shifted(block, axis, distance):
    devices = range(lax.axis_size(axis))
    route = [((i - distance) % len(devices), i) for i in devices]
    return lax.ppermute(block, axis, route)


def on_device(
    queries, keys, values, frame_ids, past_keys, past_values, block_home, windows, window_len
):
    row_count = queries.shape[0]
    feature_width = queries.shape[1]
    head_count = feature_width // HEAD_DIM
    seq_count = lax.axis_size("seq")
    my_index = lax.axis_index("seq")
    score_scale = HEAD_DIM ** (-0.5)
    query_heads = queries.reshape(row_count, head_count, HEAD_DIM)

    def attend(carried, key_rows, value_rows, key_mask):
        run_max, run_sum, run_acc = carried
        scores = (
            jnp.einsum("qhd,khd->hqk", query_heads, key_rows, preferred_element_type=jnp.float32)
            * score_scale
        )
        scores = jnp.where(key_mask[None], scores, masked_score)
        new_max = jnp.maximum(run_max, jnp.max(scores, axis=-1))
        weights = jnp.where(key_mask[None], jnp.exp(scores - new_max[..., None]), 0.0)
        rescale = jnp.exp(run_max - new_max)
        run_sum = run_sum * rescale + jnp.sum(weights, axis=-1)
        update = jnp.einsum(
            "hqk,khd->qhd",
            weights.astype(jnp.bfloat16),
            value_rows,
            preferred_element_type=jnp.float32,
        )
        run_acc = run_acc * rescale.T[..., None] + update
        return (new_max, run_sum, run_acc)

    carried = (
        jnp.full((head_count, row_count), masked_score, jnp.float32),
        jnp.zeros((head_count, row_count), jnp.float32),
        jnp.zeros((row_count, head_count, HEAD_DIM), jnp.float32),
    )
    every_frame = lax.all_gather(frame_ids, "seq", axis=0, tiled=True)
    self_mask = frame_ids[None, :] <= frame_ids[:, None]
    carried = attend(
        carried,
        keys.reshape(row_count, head_count, HEAD_DIM),
        values.reshape(row_count, head_count, HEAD_DIM),
        self_mask,
    )

    def cycle_body(offset, loop_state):
        moving, running = loop_state
        moving = shifted(moving, "seq", 1)
        source = (my_index - offset) % seq_count
        key_frames = lax.dynamic_slice_in_dim(every_frame, source * row_count, row_count, 0)
        key_mask = key_frames[None, :] <= frame_ids[:, None]
        key_rows = moving[0].reshape(row_count, head_count, HEAD_DIM)
        value_rows = moving[1].reshape(row_count, head_count, HEAD_DIM)
        running = attend(running, key_rows, value_rows, key_mask)
        return (moving, running)

    moving = jnp.stack([keys, values])
    moving, carried = lax.fori_loop(1, seq_count, cycle_body, (moving, carried))
    list_len = windows.shape[1]
    block_len = past_keys.shape[1]
    my_rows = block_home[lax.dynamic_index_in_dim(windows, my_index, 0, keepdims=False)]
    my_len = lax.dynamic_index_in_dim(window_len, my_index, 0, keepdims=False)
    live_slots = jnp.arange(list_len) < my_len
    running = carried
    piece_keys = lax.all_gather(past_keys, "seq", axis=0, tiled=True)
    piece_values = lax.all_gather(past_values, "seq", axis=0, tiled=True)
    block_count = piece_keys.shape[0]
    grouping = math.gcd(block_count, 8)
    row_ids = jnp.arange(block_count)
    member = jnp.any((row_ids[:, None] == my_rows[None, :]) & live_slots[None, :], axis=1)
    group_keys = piece_keys.reshape(
        block_count // grouping, grouping * block_len, head_count, HEAD_DIM
    )
    group_values = piece_values.reshape(
        block_count // grouping, grouping * block_len, head_count, HEAD_DIM
    )
    group_mask = jnp.repeat(member.reshape(block_count // grouping, grouping), block_len, axis=1)

    def one_group(inside, items):
        item_keys, item_values, item_mask = items
        full_mask = jnp.broadcast_to(item_mask[None, :], (row_count, item_mask.shape[0]))
        return (attend(inside, item_keys, item_values, full_mask), None)

    running, unused = lax.scan(one_group, running, (group_keys, group_values, group_mask))
    carried = running
    run_max, run_sum, run_acc = carried
    output = run_acc / run_sum.T[..., None]
    return output.reshape(row_count, feature_width).astype(jnp.bfloat16)

MESH = pl.DeviceIdType.MESH
LOG2E = 1.4426950408889634


def dot_nt(a, b):
    return lax.dot_general(a, b, (((1,), (1,)), ((), ())), preferred_element_type=jnp.float32)


def dot_tn(a, b):
    return lax.dot_general(a, b, (((0,), (0,)), ((), ())), preferred_element_type=jnp.float32)


def heads_kernel(
    q_ref,
    k_ref,
    v_ref,
    frames_ref,
    pk_ref,
    pv_ref,
    home_ref,
    windows_ref,
    len_ref,
    out_ref,
    qb,
    kb,
    vb,
    fb,
    frame_col,
    pkb,
    pvb,
    past_k,
    past_v,
    part,
    part_lse,
    got,
    got_lse,
    met,
    met_lse,
    own_acc,
    own_stat,
    ob,
    ob_met,
    q_send,
    q_recv,
    relay_send,
    kv_send,
    kv_recv,
    own_sem,
    frame_send,
    frame_recv,
    part_send,
    part_recv,
    out_send,
    out_recv,
    out_own,
    out_met,
):
    n = 4
    me = lax.axis_index("seq")
    side = lax.rem(me, 2)
    half = me // 2
    mate = me + 1 - 2 * side
    peer = lax.rem(me + 2, n)
    outer = side == half
    inner = side != half
    rows = q_ref.shape[0]
    heads_here = qb.shape[0]
    width = heads_here * HEAD_DIM
    blocks = pk_ref.shape[0]
    blk = pk_ref.shape[1]
    win = windows_ref.shape[1]
    scale = LOG2E * HEAD_DIM ** (-0.5)

    barrier = pltpu.get_barrier_semaphore()
    for t in range(1, n):
        pl.semaphore_signal(
            barrier, inc=1, device_id={"seq": lax.rem(me + t, n)}, device_id_type=MESH
        )
    pl.semaphore_wait(barrier, n - 1)

    def head_columns(which, h):
        return pl.ds(pl.multiple_of(which * width + h * HEAD_DIM, HEAD_DIM), HEAD_DIM)

    def remote(src, dst, send, recv, dest):
        return pltpu.make_async_remote_copy(
            src_ref=src,
            dst_ref=dst,
            send_sem=send,
            recv_sem=recv,
            device_id={"seq": dest},
            device_id_type=MESH,
        )

    def stationary(h, which):
        columns = head_columns(which, h)
        span = pl.ds(side * blocks, blocks)
        return [
            (k_ref.at[:, columns], kb.at[h, side]),
            (v_ref.at[:, columns], vb.at[h, side]),
            (pk_ref.at[:, :, columns], pkb.at[h, span]),
            (pv_ref.at[:, :, columns], pvb.at[h, span]),
        ]

    def kv_sends(h):
        return [
            remote(src, dst, kv_send.at[h, i], kv_recv.at[h, i], mate)
            for i, (src, dst) in enumerate(stationary(h, 1 - side))
        ]

    def q_copy(h, t):
        dest = lax.rem(me + t, n)
        columns = head_columns(lax.rem(dest, 2), h)
        return remote(q_ref.at[:, columns], qb.at[h, me], q_send.at[h, t], q_recv.at[h, t], dest)

    def direct(t):
        return jnp.logical_or(inner, lax.rem(me + t, n) != n - 1 - me)

    def unrelayed(t):
        return jnp.logical_or(outer, lax.rem(me - t + n, n) != mate)

    def relay_copy(h):
        dest = n - 1 - mate
        t = lax.rem(dest - mate + n, n)
        return remote(qb.at[h, mate], qb.at[h, mate], relay_send.at[h], q_recv.at[h, t], dest)

    def relay(h):
        @pl.when(inner)
        def _():
            q_copy(h, lax.rem(me - mate + n, n)).wait_recv()
            relay_copy(h).start()

    def owns(h):
        mine = stationary(h, side) + [(q_ref.at[:, head_columns(side, h)], qb.at[h, me])]
        return [
            pltpu.make_async_copy(src, dst, own_sem.at[h, i]) for i, (src, dst) in enumerate(mine)
        ]

    def frame_send_of(t):
        return remote(
            frames_ref, fb.at[me], frame_send.at[t], frame_recv.at[t], lax.rem(me + t, n)
        )

    def start(h):
        for t in (1, 3, 2):
            pl.when(direct(t))(q_copy(h, t).start)
        for copy in kv_sends(h):
            copy.start()
        for copy in owns(h):
            copy.start()

    def both(h, i, src, dst, dst_lse, where, dest):
        return [
            remote(part.at[h, src], dst.at[h, where], part_send.at[h, i, 0], part_recv.at[h, i, 0], dest),
            remote(part_lse.at[h, src], dst_lse.at[h, where], part_send.at[h, i, 1], part_recv.at[h, i, 1], dest),
        ]

    def far_outer(h):
        return both(h, 0, 1 - half, got, got_lse, 1 - half, peer)

    def far_inner_by_outer(h):
        return both(h, 1, half, got, got_lse, half, peer)

    def far_inner_by_inner(h):
        return both(h, 2, half, met, met_lse, 1, n - 1 - me)

    def near_inner_by_outer(h):
        return both(h, 3, 2, met, met_lse, 0, mate)

    def out_copy(h):
        return remote(
            ob.at[h, 1 - side],
            out_ref.at[:, head_columns(side, h)],
            out_send.at[h],
            out_recv.at[h],
            mate,
        )

    def out_own_copy(h):
        return pltpu.make_async_copy(
            ob.at[h, side], out_ref.at[:, head_columns(side, h)], out_own.at[h]
        )

    def out_met_copy(h):
        return pltpu.make_async_copy(
            ob_met.at[h], out_ref.at[:, head_columns(1 - side, h)], out_met.at[h]
        )

    for t in range(1, n):
        frame_send_of(t).start()
    start(0)
    start(1)
    fb[me] = frames_ref[...]
    for t in range(1, n):
        frame_send_of(t).wait()
    for s in range(n):
        frame_col[s] = jnp.transpose(fb[s])
    relay(0)

    def attend(h, g, s):
        query = qb[h, s]
        state = (
            jnp.full((1, rows), -1e30, jnp.float32),
            jnp.zeros((1, rows), jnp.float32),
            jnp.zeros((HEAD_DIM, rows), jnp.float32),
        )

        def update(state, key, value, allowed):
            top, total, acc = state
            score = dot_nt(key, query) * scale
            if allowed is not None:
                score = jnp.where(allowed, score, -1e30)
            new_top = jnp.maximum(top, jnp.max(score, axis=0, keepdims=True))
            weight = jnp.exp2(score - new_top)
            fade = jnp.exp2(top - new_top)
            total = total * fade + jnp.sum(weight, axis=0, keepdims=True)
            acc = acc * fade + dot_tn(value, weight.astype(jnp.bfloat16))
            return new_top, total, acc

        query_frame = fb[s, 0:1, :]
        for i in range(2):
            j = 2 * g + i
            if j <= s + 1:
                allowed = frame_col[j][:, 0:1] <= query_frame if j >= s else None
                state = update(state, kb[h, i], vb[h, i], allowed)
        keys, values = [], []
        slot = lax.broadcasted_iota(jnp.int32, (win * blk, 1), 0) // blk
        live = jnp.zeros((win * blk, 1), jnp.int32)
        for w in range(win):
            row = home_ref[windows_ref[s, w]]
            keys.append(past_k[lax.rem(row, 2 * blocks)])
            values.append(past_v[lax.rem(row, 2 * blocks)])
            here = (row // (2 * blocks) == g) & (w < len_ref[s])
            live = jnp.where(slot == w, here.astype(jnp.int32), live)
        return update(
            state, jnp.concatenate(keys, axis=0), jnp.concatenate(values, axis=0), live > 0
        )

    def merge_own(h, k):
        top, total = own_stat[h, k, 0:1], own_stat[h, k, 1:2]
        other = got_lse[h, k]
        new_top = jnp.maximum(top, other)
        mine, theirs = jnp.exp2(top - new_top), jnp.exp2(other - new_top)
        mixed = own_acc[h, k] * mine + got[h, k].astype(jnp.float32) * theirs
        ob[h, k] = jnp.transpose(mixed / (total * mine + theirs)).astype(jnp.bfloat16)

    def merge_met(h):
        one, two = met_lse[h, 0], met_lse[h, 1]
        top = jnp.maximum(one, two)
        one, two = jnp.exp2(one - top), jnp.exp2(two - top)
        mixed = met[h, 0].astype(jnp.float32) * one + met[h, 1].astype(jnp.float32) * two
        ob_met[h] = jnp.transpose(mixed / (one + two)).astype(jnp.bfloat16)

    def merge(h):
        for copy in both(h, 0, 0, got, got_lse, half, peer):
            copy.wait_recv()
        merge_own(h, half)

        @pl.when(outer)
        def _():
            out_own_copy(h).start()

        @pl.when(inner)
        def _():
            out_copy(h).start()
            for copy in both(h, 1, 0, got, got_lse, 1 - half, peer):
                copy.wait_recv()
            merge_own(h, 1 - half)
            out_own_copy(h).start()
            for copy in far_inner_by_inner(h) + near_inner_by_outer(h):
                copy.wait_recv()
            merge_met(h)
            out_met_copy(h).start()

    def one_head(h, carry):
        for t in range(1, n):
            pl.when(unrelayed(t))(q_copy(h, t).wait_recv)
        for copy in kv_sends(h):
            copy.wait_recv()
        for copy in owns(h):
            copy.wait()

        @pl.when(h + 2 < heads_here)
        def _():
            start(h + 2)

        past_k[...] = pkb[h]
        past_v[...] = pvb[h]

        def away(g):
            for k in range(2):
                top, total, acc = attend(h, g, 2 * (1 - g) + k)
                part[h, k] = (acc / total).astype(jnp.bfloat16)
                part_lse[h, k] = top + jnp.log2(total)

        def home(g):
            for k in range(2):
                top, total, acc = attend(h, g, 2 * g + k)
                own_acc[h, k] = acc
                own_stat[h, k, 0:1] = top
                own_stat[h, k, 1:2] = total
                if k != g:
                    part[h, 2] = (acc / total).astype(jnp.bfloat16)
                    part_lse[h, 2] = top + jnp.log2(total)

        for g in range(2):
            pl.when(half == g)(functools.partial(away, g))
        for copy in far_outer(h):
            copy.start()

        @pl.when(outer)
        def _():
            for copy in far_inner_by_outer(h):
                copy.start()

        @pl.when(inner)
        def _():
            for copy in far_inner_by_inner(h):
                copy.start()

        @pl.when(h + 1 < heads_here)
        def _():
            relay(h + 1)

        for g in range(2):
            pl.when(half == g)(functools.partial(home, g))

        @pl.when(outer)
        def _():
            for copy in near_inner_by_outer(h):
                copy.start()

        @pl.when(h > 0)
        def _():
            merge(h - 1)

        return carry

    lax.fori_loop(0, heads_here, one_head, 0)
    merge(heads_here - 1)

    def finish(h, carry):
        for t in range(1, n):
            pl.when(direct(t))(q_copy(h, t).wait_send)
        for copy in kv_sends(h) + far_outer(h):
            copy.wait_send()
        out_own_copy(h).wait()

        @pl.when(outer)
        def _():
            for copy in far_inner_by_outer(h) + near_inner_by_outer(h):
                copy.wait_send()
            out_copy(h).wait_recv()

        @pl.when(inner)
        def _():
            relay_copy(h).wait_send()
            for copy in far_inner_by_inner(h):
                copy.wait_send()
            out_copy(h).wait_send()
            out_met_copy(h).wait()

        return carry

    lax.fori_loop(0, heads_here, finish, 0)


def by_heads(
    queries, keys, values, frame_ids, past_keys, past_values, block_home, windows, window_len
):
    n = lax.axis_size("seq")
    rows, features = queries.shape
    heads_here = features // HEAD_DIM // 2
    blocks, blk = past_keys.shape[0], past_keys.shape[1]
    frames = jnp.broadcast_to(frame_ids[None, :].astype(jnp.float32), (8, rows))
    anywhere = pl.BlockSpec(memory_space=pl.ANY)
    vmem = pl.BlockSpec(memory_space=pltpu.VMEM)
    smem = pl.BlockSpec(memory_space=pltpu.SMEM)
    dma = pltpu.SemaphoreType.DMA
    bf16, f32 = jnp.bfloat16, jnp.float32
    return pl.pallas_call(
        heads_kernel,
        out_shape=jax.ShapeDtypeStruct((rows, features), bf16),
        in_specs=[anywhere] * 3 + [vmem] + [anywhere] * 2 + [smem] * 3,
        out_specs=anywhere,
        scratch_shapes=[
            pltpu.VMEM((heads_here, n, rows, HEAD_DIM), bf16),
            pltpu.VMEM((heads_here, 2, rows, HEAD_DIM), bf16),
            pltpu.VMEM((heads_here, 2, rows, HEAD_DIM), bf16),
            pltpu.VMEM((n, 8, rows), f32),
            pltpu.VMEM((n, rows, 8), f32),
            pltpu.VMEM((heads_here, 2 * blocks, blk, HEAD_DIM), bf16),
            pltpu.VMEM((heads_here, 2 * blocks, blk, HEAD_DIM), bf16),
            pltpu.VMEM((2 * blocks, blk, HEAD_DIM), bf16),
            pltpu.VMEM((2 * blocks, blk, HEAD_DIM), bf16),
            pltpu.VMEM((heads_here, 3, HEAD_DIM, rows), bf16),
            pltpu.VMEM((heads_here, 3, 1, rows), f32),
            pltpu.VMEM((heads_here, 2, HEAD_DIM, rows), bf16),
            pltpu.VMEM((heads_here, 2, 1, rows), f32),
            pltpu.VMEM((heads_here, 2, HEAD_DIM, rows), bf16),
            pltpu.VMEM((heads_here, 2, 1, rows), f32),
            pltpu.VMEM((heads_here, 2, HEAD_DIM, rows), f32),
            pltpu.VMEM((heads_here, 2, 2, rows), f32),
            pltpu.VMEM((heads_here, 2, rows, HEAD_DIM), bf16),
            pltpu.VMEM((heads_here, rows, HEAD_DIM), bf16),
            dma((heads_here, n)),
            dma((heads_here, n)),
            dma((heads_here,)),
            dma((heads_here, 4)),
            dma((heads_here, 4)),
            dma((heads_here, 5)),
            dma((n,)),
            dma((n,)),
            dma((heads_here, 4, 2)),
            dma((heads_here, 4, 2)),
            dma((heads_here,)),
            dma((heads_here,)),
            dma((heads_here,)),
            dma((heads_here,)),
        ],
        compiler_params=pltpu.CompilerParams(
            collective_id=0, has_side_effects=True, vmem_limit_bytes=48 * 1024 * 1024
        ),
    )(queries, keys, values, frames, past_keys, past_values, block_home, windows, window_len)


def pick(queries, *rest):
    heads = queries.shape[1] // HEAD_DIM
    if lax.axis_size("seq") == 4 and heads % 2 == 0 and heads >= 6:
        return by_heads(queries, *rest)
    return on_device(queries, *rest)


def solution(mesh):
    in_specs = (
        P(("clips", "seq"), ("cache", "head")),
        P(("clips", "seq"), ("cache", "head")),
        P(("clips", "seq"), ("cache", "head")),
        P(("clips", "seq")),
        P(("clips", "seq"), None, ("cache", "head")),
        P(("clips", "seq"), None, ("cache", "head")),
        P("clips"),
        P("clips", None),
        P("clips"),
    )
    out_specs = P(("clips", "seq"), ("cache", "head"))
    return jax.shard_map(
        pick, mesh=mesh, in_specs=in_specs, out_specs=out_specs, check_vma=False
    )
```

```python
import functools
import math

import jax
import jax.numpy as jnp
from jax import lax
from jax.experimental import pallas as pl
from jax.experimental.pallas import tpu as pltpu
from jax.sharding import PartitionSpec as P

HEAD_DIM = 128


masked_score = -1e30


def shifted(block, axis, distance):
    devices = range(lax.axis_size(axis))
    route = [((i - distance) % len(devices), i) for i in devices]
    return lax.ppermute(block, axis, route)


def on_device(
    queries, keys, values, frame_ids, past_keys, past_values, block_home, windows, window_len
):
    row_count = queries.shape[0]
    feature_width = queries.shape[1]
    head_count = feature_width // HEAD_DIM
    seq_count = lax.axis_size("seq")
    my_index = lax.axis_index("seq")
    score_scale = HEAD_DIM ** (-0.5)
    query_heads = queries.reshape(row_count, head_count, HEAD_DIM)

    def attend(carried, key_rows, value_rows, key_mask):
        run_max, run_sum, run_acc = carried
        scores = (
            jnp.einsum("qhd,khd->hqk", query_heads, key_rows, preferred_element_type=jnp.float32)
            * score_scale
        )
        scores = jnp.where(key_mask[None], scores, masked_score)
        new_max = jnp.maximum(run_max, jnp.max(scores, axis=-1))
        weights = jnp.where(key_mask[None], jnp.exp(scores - new_max[..., None]), 0.0)
        rescale = jnp.exp(run_max - new_max)
        run_sum = run_sum * rescale + jnp.sum(weights, axis=-1)
        update = jnp.einsum(
            "hqk,khd->qhd",
            weights.astype(jnp.bfloat16),
            value_rows,
            preferred_element_type=jnp.float32,
        )
        run_acc = run_acc * rescale.T[..., None] + update
        return (new_max, run_sum, run_acc)

    carried = (
        jnp.full((head_count, row_count), masked_score, jnp.float32),
        jnp.zeros((head_count, row_count), jnp.float32),
        jnp.zeros((row_count, head_count, HEAD_DIM), jnp.float32),
    )
    every_frame = lax.all_gather(frame_ids, "seq", axis=0, tiled=True)
    self_mask = frame_ids[None, :] <= frame_ids[:, None]
    carried = attend(
        carried,
        keys.reshape(row_count, head_count, HEAD_DIM),
        values.reshape(row_count, head_count, HEAD_DIM),
        self_mask,
    )

    def cycle_body(offset, loop_state):
        moving, running = loop_state
        moving = shifted(moving, "seq", 1)
        source = (my_index - offset) % seq_count
        key_frames = lax.dynamic_slice_in_dim(every_frame, source * row_count, row_count, 0)
        key_mask = key_frames[None, :] <= frame_ids[:, None]
        key_rows = moving[0].reshape(row_count, head_count, HEAD_DIM)
        value_rows = moving[1].reshape(row_count, head_count, HEAD_DIM)
        running = attend(running, key_rows, value_rows, key_mask)
        return (moving, running)

    moving = jnp.stack([keys, values])
    moving, carried = lax.fori_loop(1, seq_count, cycle_body, (moving, carried))
    list_len = windows.shape[1]
    block_len = past_keys.shape[1]
    my_rows = block_home[lax.dynamic_index_in_dim(windows, my_index, 0, keepdims=False)]
    my_len = lax.dynamic_index_in_dim(window_len, my_index, 0, keepdims=False)
    live_slots = jnp.arange(list_len) < my_len
    running = carried
    piece_keys = lax.all_gather(past_keys, "seq", axis=0, tiled=True)
    piece_values = lax.all_gather(past_values, "seq", axis=0, tiled=True)
    block_count = piece_keys.shape[0]
    grouping = math.gcd(block_count, 8)
    row_ids = jnp.arange(block_count)
    member = jnp.any((row_ids[:, None] == my_rows[None, :]) & live_slots[None, :], axis=1)
    group_keys = piece_keys.reshape(
        block_count // grouping, grouping * block_len, head_count, HEAD_DIM
    )
    group_values = piece_values.reshape(
        block_count // grouping, grouping * block_len, head_count, HEAD_DIM
    )
    group_mask = jnp.repeat(member.reshape(block_count // grouping, grouping), block_len, axis=1)

    def one_group(inside, items):
        item_keys, item_values, item_mask = items
        full_mask = jnp.broadcast_to(item_mask[None, :], (row_count, item_mask.shape[0]))
        return (attend(inside, item_keys, item_values, full_mask), None)

    running, unused = lax.scan(one_group, running, (group_keys, group_values, group_mask))
    carried = running
    run_max, run_sum, run_acc = carried
    output = run_acc / run_sum.T[..., None]
    return output.reshape(row_count, feature_width).astype(jnp.bfloat16)

MESH = pl.DeviceIdType.MESH
LOG2E = 1.4426950408889634


def dot_nt(a, b):
    return lax.dot_general(a, b, (((1,), (1,)), ((), ())), preferred_element_type=jnp.float32)


def dot_tn(a, b):
    return lax.dot_general(a, b, (((0,), (0,)), ((), ())), preferred_element_type=jnp.float32)


def heads_kernel(
    q_ref,
    k_ref,
    v_ref,
    frames_ref,
    pk_ref,
    pv_ref,
    home_ref,
    windows_ref,
    len_ref,
    out_ref,
    qb,
    kb,
    vb,
    fb,
    frame_col,
    pkb,
    pvb,
    past_k,
    past_v,
    part,
    part_lse,
    got,
    got_lse,
    met,
    met_lse,
    own_acc,
    own_stat,
    ob,
    ob_met,
    q_send,
    q_recv,
    relay_send,
    kv_send,
    kv_recv,
    own_sem,
    frame_send,
    frame_recv,
    part_send,
    part_recv,
    out_send,
    out_recv,
    out_own,
    out_met,
):
    n = 4
    me = lax.axis_index("seq")
    side = lax.rem(me, 2)
    half = me // 2
    mate = me + 1 - 2 * side
    peer = lax.rem(me + 2, n)
    outer = side == half
    inner = side != half
    rows = q_ref.shape[0]
    heads_here = qb.shape[0]
    width = heads_here * HEAD_DIM
    blocks = pk_ref.shape[0]
    blk = pk_ref.shape[1]
    win = windows_ref.shape[1]
    scale = LOG2E * HEAD_DIM ** (-0.5)

    barrier = pltpu.get_barrier_semaphore()
    for t in range(1, n):
        pl.semaphore_signal(
            barrier, inc=1, device_id={"seq": lax.rem(me + t, n)}, device_id_type=MESH
        )
    pl.semaphore_wait(barrier, n - 1)

    def head_columns(which, h):
        return pl.ds(pl.multiple_of(which * width + h * HEAD_DIM, HEAD_DIM), HEAD_DIM)

    def remote(src, dst, send, recv, dest):
        return pltpu.make_async_remote_copy(
            src_ref=src,
            dst_ref=dst,
            send_sem=send,
            recv_sem=recv,
            device_id={"seq": dest},
            device_id_type=MESH,
        )

    def stationary(h, which):
        columns = head_columns(which, h)
        span = pl.ds(side * blocks, blocks)
        return [
            (k_ref.at[:, columns], kb.at[h, side]),
            (v_ref.at[:, columns], vb.at[h, side]),
            (pk_ref.at[:, :, columns], pkb.at[h, span]),
            (pv_ref.at[:, :, columns], pvb.at[h, span]),
        ]

    def kv_sends(h):
        return [
            remote(src, dst, kv_send.at[h, i], kv_recv.at[h, i], mate)
            for i, (src, dst) in enumerate(stationary(h, 1 - side))
        ]

    def q_copy(h, t):
        dest = lax.rem(me + t, n)
        columns = head_columns(lax.rem(dest, 2), h)
        return remote(q_ref.at[:, columns], qb.at[h, me], q_send.at[h, t], q_recv.at[h, t], dest)

    def direct(t):
        return jnp.logical_or(inner, lax.rem(me + t, n) != n - 1 - me)

    def unrelayed(t):
        return jnp.logical_or(outer, lax.rem(me - t + n, n) != mate)

    def relay_copy(h):
        dest = n - 1 - mate
        t = lax.rem(dest - mate + n, n)
        return remote(qb.at[h, mate], qb.at[h, mate], relay_send.at[h], q_recv.at[h, t], dest)

    def relay(h):
        @pl.when(inner)
        def _():
            q_copy(h, lax.rem(me - mate + n, n)).wait_recv()
            relay_copy(h).start()

    def owns(h):
        mine = stationary(h, side) + [(q_ref.at[:, head_columns(side, h)], qb.at[h, me])]
        return [
            pltpu.make_async_copy(src, dst, own_sem.at[h, i]) for i, (src, dst) in enumerate(mine)
        ]

    def frame_send_of(t):
        return remote(
            frames_ref, fb.at[me], frame_send.at[t], frame_recv.at[t], lax.rem(me + t, n)
        )

    def start(h):
        for t in (1, 3, 2):
            pl.when(direct(t))(q_copy(h, t).start)
        for copy in kv_sends(h):
            copy.start()
        for copy in owns(h):
            copy.start()

    def both(h, i, src, dst, dst_lse, where, dest):
        return [
            remote(part.at[h, src], dst.at[h, where], part_send.at[h, i, 0], part_recv.at[h, i, 0], dest),
            remote(part_lse.at[h, src], dst_lse.at[h, where], part_send.at[h, i, 1], part_recv.at[h, i, 1], dest),
        ]

    def far_outer(h):
        return both(h, 0, 1 - half, got, got_lse, 1 - half, peer)

    def far_inner_by_outer(h):
        return both(h, 1, half, got, got_lse, half, peer)

    def far_inner_by_inner(h):
        return both(h, 2, half, met, met_lse, 1, n - 1 - me)

    def near_inner_by_outer(h):
        return both(h, 3, 2, met, met_lse, 0, mate)

    def out_copy(h):
        return remote(
            ob.at[h, 1 - side],
            out_ref.at[:, head_columns(side, h)],
            out_send.at[h],
            out_recv.at[h],
            mate,
        )

    def out_own_copy(h):
        return pltpu.make_async_copy(
            ob.at[h, side], out_ref.at[:, head_columns(side, h)], out_own.at[h]
        )

    def out_met_copy(h):
        return pltpu.make_async_copy(
            ob_met.at[h], out_ref.at[:, head_columns(1 - side, h)], out_met.at[h]
        )

    for t in range(1, n):
        frame_send_of(t).start()
    start(0)
    start(1)
    fb[me] = frames_ref[...]
    for t in range(1, n):
        frame_send_of(t).wait()
    for s in range(n):
        frame_col[s] = jnp.transpose(fb[s])
    relay(0)

    def attend(h, g, s):
        query = qb[h, s]
        state = (
            jnp.full((1, rows), -1e30, jnp.float32),
            jnp.zeros((1, rows), jnp.float32),
            jnp.zeros((HEAD_DIM, rows), jnp.float32),
        )

        def update(state, key, value, allowed):
            top, total, acc = state
            score = dot_nt(key, query) * scale
            if allowed is not None:
                score = jnp.where(allowed, score, -1e30)
            new_top = jnp.maximum(top, jnp.max(score, axis=0, keepdims=True))
            weight = jnp.exp2(score - new_top)
            fade = jnp.exp2(top - new_top)
            total = total * fade + jnp.sum(weight, axis=0, keepdims=True)
            acc = acc * fade + dot_tn(value, weight.astype(jnp.bfloat16))
            return new_top, total, acc

        query_frame = fb[s, 0:1, :]
        for i in range(2):
            j = 2 * g + i
            if j <= s + 1:
                allowed = frame_col[j][:, 0:1] <= query_frame if j >= s else None
                state = update(state, kb[h, i], vb[h, i], allowed)
        keys, values = [], []
        slot = lax.broadcasted_iota(jnp.int32, (win * blk, 1), 0) // blk
        live = jnp.zeros((win * blk, 1), jnp.int32)
        for w in range(win):
            row = home_ref[windows_ref[s, w]]
            keys.append(past_k[lax.rem(row, 2 * blocks)])
            values.append(past_v[lax.rem(row, 2 * blocks)])
            here = (row // (2 * blocks) == g) & (w < len_ref[s])
            live = jnp.where(slot == w, here.astype(jnp.int32), live)
        return update(
            state, jnp.concatenate(keys, axis=0), jnp.concatenate(values, axis=0), live > 0
        )

    def merge_own(h, k):
        top, total = own_stat[h, k, 0:1], own_stat[h, k, 1:2]
        other = got_lse[h, k]
        new_top = jnp.maximum(top, other)
        mine, theirs = jnp.exp2(top - new_top), jnp.exp2(other - new_top)
        mixed = own_acc[h, k] * mine + got[h, k].astype(jnp.float32) * theirs
        ob[h, k] = jnp.transpose(mixed / (total * mine + theirs)).astype(jnp.bfloat16)

    def merge_met(h):
        one, two = met_lse[h, 0], met_lse[h, 1]
        top = jnp.maximum(one, two)
        one, two = jnp.exp2(one - top), jnp.exp2(two - top)
        mixed = met[h, 0].astype(jnp.float32) * one + met[h, 1].astype(jnp.float32) * two
        ob_met[h] = jnp.transpose(mixed / (one + two)).astype(jnp.bfloat16)

    def merge(h):
        for copy in both(h, 0, 0, got, got_lse, half, peer):
            copy.wait_recv()
        merge_own(h, half)

        @pl.when(outer)
        def _():
            out_own_copy(h).start()

        @pl.when(inner)
        def _():
            out_copy(h).start()
            for copy in both(h, 1, 0, got, got_lse, 1 - half, peer):
                copy.wait_recv()
            merge_own(h, 1 - half)
            out_own_copy(h).start()
            for copy in far_inner_by_inner(h) + near_inner_by_outer(h):
                copy.wait_recv()
            merge_met(h)
            out_met_copy(h).start()

    def one_head(h, carry):
        for t in range(1, n):
            pl.when(unrelayed(t))(q_copy(h, t).wait_recv)
        for copy in kv_sends(h):
            copy.wait_recv()
        for copy in owns(h):
            copy.wait()

        past_k[...] = pkb[h]
        past_v[...] = pvb[h]

        def away(g):
            for k in range(2):
                top, total, acc = attend(h, g, 2 * (1 - g) + k)
                part[h, k] = (acc / total).astype(jnp.bfloat16)
                part_lse[h, k] = top + jnp.log2(total)

        def home(g):
            for k in range(2):
                top, total, acc = attend(h, g, 2 * g + k)
                own_acc[h, k] = acc
                own_stat[h, k, 0:1] = top
                own_stat[h, k, 1:2] = total
                if k != g:
                    part[h, 2] = (acc / total).astype(jnp.bfloat16)
                    part_lse[h, 2] = top + jnp.log2(total)

        for g in range(2):
            pl.when(half == g)(functools.partial(away, g))
        for copy in far_outer(h):
            copy.start()

        @pl.when(outer)
        def _():
            for copy in far_inner_by_outer(h):
                copy.start()

        @pl.when(inner)
        def _():
            for copy in far_inner_by_inner(h):
                copy.start()

        @pl.when(h + 1 < heads_here)
        def _():
            relay(h + 1)

        @pl.when(h + 2 < heads_here)
        def _():
            start(h + 2)

        for g in range(2):
            pl.when(half == g)(functools.partial(home, g))

        @pl.when(outer)
        def _():
            for copy in near_inner_by_outer(h):
                copy.start()

        @pl.when(h > 0)
        def _():
            merge(h - 1)

        return carry

    lax.fori_loop(0, heads_here, one_head, 0)
    merge(heads_here - 1)

    def finish(h, carry):
        for t in range(1, n):
            pl.when(direct(t))(q_copy(h, t).wait_send)
        for copy in kv_sends(h) + far_outer(h):
            copy.wait_send()
        out_own_copy(h).wait()

        @pl.when(outer)
        def _():
            for copy in far_inner_by_outer(h) + near_inner_by_outer(h):
                copy.wait_send()
            out_copy(h).wait_recv()

        @pl.when(inner)
        def _():
            relay_copy(h).wait_send()
            for copy in far_inner_by_inner(h):
                copy.wait_send()
            out_copy(h).wait_send()
            out_met_copy(h).wait()

        return carry

    lax.fori_loop(0, heads_here, finish, 0)


def by_heads(
    queries, keys, values, frame_ids, past_keys, past_values, block_home, windows, window_len
):
    n = lax.axis_size("seq")
    rows, features = queries.shape
    heads_here = features // HEAD_DIM // 2
    blocks, blk = past_keys.shape[0], past_keys.shape[1]
    frames = jnp.broadcast_to(frame_ids[None, :].astype(jnp.float32), (8, rows))
    anywhere = pl.BlockSpec(memory_space=pl.ANY)
    vmem = pl.BlockSpec(memory_space=pltpu.VMEM)
    smem = pl.BlockSpec(memory_space=pltpu.SMEM)
    dma = pltpu.SemaphoreType.DMA
    bf16, f32 = jnp.bfloat16, jnp.float32
    return pl.pallas_call(
        heads_kernel,
        out_shape=jax.ShapeDtypeStruct((rows, features), bf16),
        in_specs=[anywhere] * 3 + [vmem] + [anywhere] * 2 + [smem] * 3,
        out_specs=anywhere,
        scratch_shapes=[
            pltpu.VMEM((heads_here, n, rows, HEAD_DIM), bf16),
            pltpu.VMEM((heads_here, 2, rows, HEAD_DIM), bf16),
            pltpu.VMEM((heads_here, 2, rows, HEAD_DIM), bf16),
            pltpu.VMEM((n, 8, rows), f32),
            pltpu.VMEM((n, rows, 8), f32),
            pltpu.VMEM((heads_here, 2 * blocks, blk, HEAD_DIM), bf16),
            pltpu.VMEM((heads_here, 2 * blocks, blk, HEAD_DIM), bf16),
            pltpu.VMEM((2 * blocks, blk, HEAD_DIM), bf16),
            pltpu.VMEM((2 * blocks, blk, HEAD_DIM), bf16),
            pltpu.VMEM((heads_here, 3, HEAD_DIM, rows), bf16),
            pltpu.VMEM((heads_here, 3, 1, rows), f32),
            pltpu.VMEM((heads_here, 2, HEAD_DIM, rows), bf16),
            pltpu.VMEM((heads_here, 2, 1, rows), f32),
            pltpu.VMEM((heads_here, 2, HEAD_DIM, rows), bf16),
            pltpu.VMEM((heads_here, 2, 1, rows), f32),
            pltpu.VMEM((heads_here, 2, HEAD_DIM, rows), f32),
            pltpu.VMEM((heads_here, 2, 2, rows), f32),
            pltpu.VMEM((heads_here, 2, rows, HEAD_DIM), bf16),
            pltpu.VMEM((heads_here, rows, HEAD_DIM), bf16),
            dma((heads_here, n)),
            dma((heads_here, n)),
            dma((heads_here,)),
            dma((heads_here, 4)),
            dma((heads_here, 4)),
            dma((heads_here, 5)),
            dma((n,)),
            dma((n,)),
            dma((heads_here, 4, 2)),
            dma((heads_here, 4, 2)),
            dma((heads_here,)),
            dma((heads_here,)),
            dma((heads_here,)),
            dma((heads_here,)),
        ],
        compiler_params=pltpu.CompilerParams(
            collective_id=0, has_side_effects=True, vmem_limit_bytes=48 * 1024 * 1024
        ),
    )(queries, keys, values, frames, past_keys, past_values, block_home, windows, window_len)


def pick(queries, *rest):
    heads = queries.shape[1] // HEAD_DIM
    if lax.axis_size("seq") == 4 and heads % 2 == 0 and heads >= 6:
        return by_heads(queries, *rest)
    return on_device(queries, *rest)


def solution(mesh):
    in_specs = (
        P(("clips", "seq"), ("cache", "head")),
        P(("clips", "seq"), ("cache", "head")),
        P(("clips", "seq"), ("cache", "head")),
        P(("clips", "seq")),
        P(("clips", "seq"), None, ("cache", "head")),
        P(("clips", "seq"), None, ("cache", "head")),
        P("clips"),
        P("clips", None),
        P("clips"),
    )
    out_specs = P(("clips", "seq"), ("cache", "head"))
    return jax.shard_map(
        pick, mesh=mesh, in_specs=in_specs, out_specs=out_specs, check_vma=False
    )
```
